32 devices in a mesh: grp: 2 (over x), date: 16 (over z, y, core).
Axes of the slice: x: 2, y: 2, z: 4, core: 2. Of those that a mesh axis runs over, the one named last changes fastest.
Arguments:
- slc: bfloat16 [96, 2, 16, 512], P('date', None, 'grp'), parts along dimension 2, may hold values from -30 to 30
- line_mask: int32 [96, 16], P('date', 'grp'), parts along dimension 1, may hold values 0 or 1
- pair_dev: int32 [400, 2], P('date'), may hold values from 0 to 15, all different within a row; in each aligned block of 25 rows (0 to 24, 25 to 49, ...) at most 5 rows name the same one
- pair_slot: int32 [400, 2], P('date'), may hold values from 0 to 5
Outputs:
- solution: float32 [96, 16, 512], P('date', 'grp'), parts along dimension 1
- residual: float32 [96, 16, 512], P('date', 'grp'), parts along dimension 1
The draws below stay inside these ranges and needn't reach their ends.
There are 2 independent parts, one for each index of `grp`. The reference program is written for one: setup_inputs(seed, part) draws one part's arguments, and reference() takes and returns one part's arrays. A program takes and returns all parts, laid end to end along the dimension named above; an argument that names none is the same for every part. Nothing has to cross between parts.
Inputs may be any that keep to these rules, and one draw needn't show every extreme that they name: `pair_dev`: of the 25 rows held by one device of date, at most 5 name any one device; some device is named by exactly 5 of them; the two columns of a row differ.
All inputs are finite; a program needn't handle non-finite values. No bound on the sum of `line_mask` on one device may be relied on, other than what follows from the above.
Results may differ from the reference program's by a relative error of at most 0.0003.
Values may be sent and summed in bfloat16 or wider, within the bound.
No kernel may reach another device: no remote copies, remote signals or barrier semaphores. Data moves between devices by JAX's collectives and lax.ppermute only.
A program may use at most 128 MiB of HBM per device.

```python
import math
import jax
import jax.numpy as jnp
import numpy as np
from jax import lax

ACQ_DEV = 6
PAIR_DEV = 25
ROWS = 8
COLS = 512
ITERS = 2
N_ACQ = 96
PAIRS = 400
DATE_DEVS = 16
CAP = 5


def draw_slc(key, part):
    keys = jax.random.split(key, 7)
    shape = (N_ACQ, ROWS, COLS)
    base_real = 0.7 * jax.random.normal(keys[0], (ROWS, COLS), jnp.float32)
    base_imag = 0.7 * jax.random.normal(keys[6], (ROWS, COLS), jnp.float32)
    offsets = jax.random.uniform(keys[2], (N_ACQ, 1, 1), jnp.float32, -1.2, 1.2)
    ramps = jax.random.uniform(keys[3], (N_ACQ, 1, 1), jnp.float32, -1.0, 1.0)
    columns = jnp.arange(COLS, dtype=jnp.float32) * (2.0 / COLS) - 1.0
    phase = offsets + ramps * columns[None, None, :] + 0.3 * jax.random.normal(keys[4], shape, jnp.float32)
    sigma = jnp.exp(jax.random.uniform(keys[5], (N_ACQ, 1, 1), jnp.float32, math.log(0.2), 0.0))
    noise = jax.random.normal(keys[1], (2,) + shape, jnp.float32)
    cosine = jnp.cos(phase)
    sine = jnp.sin(phase)
    real_part = base_real[None] * cosine - base_imag[None] * sine + sigma * noise[0]
    imag_part = base_real[None] * sine + base_imag[None] * cosine + sigma * noise[1]
    stacked = jnp.stack([real_part, imag_part], axis=1)
    return jnp.clip(stacked, -30.0, 30.0).astype(jnp.bfloat16)


def with_ends(entries, rng, least, high):
    dims = entries.shape
    place = [jax.random.randint(jax.random.fold_in(rng, axis), (), 0, dims[axis]) for axis in range(len(dims))]
    entries = entries.at[tuple(place)].set(least)
    longest = dims.index(max(dims))
    place[longest] = (place[longest] + 1) % dims[longest]
    return entries.at[tuple(place)].set(high)


def routed_block(own_key, own, number, rows, number_of, top, reach, lean):
    sequence = jax.random.permutation(own_key, number_of)
    packed, ordinary = portions_of(number_of, rows * top, reach, lean, True), portions_of(number_of, rows * top, reach, lean, False)
    places = jnp.arange(number_of)

    def named(tallies, turn):
        used = int((tallies > 0).sum())
        fixed = max(1, used // 4)
        passed = fixed + (places - fixed + turn * (used - fixed)) % max(1, number_of - fixed)
        return jnp.zeros((number_of,), jnp.int32).at[sequence[jnp.where(places < fixed, places, passed)]].set(jnp.asarray(tallies, jnp.int32))

    tallies = jnp.where(number % 4 == 0, named(packed, number // 4), named(ordinary, number - number // 4 - 1))
    mixed = jax.random.permutation(jax.random.fold_in(own, 3), number_of)
    donor, receiver = mixed[0:number_of // 2 * 2:2], mixed[1:number_of // 2 * 2:2]
    room = jnp.minimum(tallies[donor] - 1, reach - tallies[receiver]) // 2
    room = jnp.where((donor == sequence[0]) | (receiver == sequence[0]) | (tallies[receiver] == 0), 0, jnp.maximum(room, 0))
    passed = jax.random.randint(jax.random.fold_in(own, 4), (number_of // 2,), 0, 1 << 20) % (room + 1)
    tallies = tallies.at[donor].add(-passed).at[receiver].add(passed)
    items = jnp.searchsorted(jnp.cumsum(tallies), jnp.arange(rows * top), side="right").astype(jnp.int32)
    table = items.reshape(top, rows).T
    table = table[jax.random.permutation(jax.random.fold_in(own, 1), rows)]
    turn = jax.random.randint(jax.random.fold_in(own, 2), (rows, 1), 0, top)
    return jnp.take_along_axis(table, (jnp.arange(top)[None, :] + turn) % top, axis=1)


def portions_of(number_of, total, reach, lean, full):
    loads = [(1 << 20) // math.isqrt(grade ** lean) + 1 for grade in range(1, number_of + 1)]
    largest = reach if full else min(reach, max(-(-total // number_of), total * loads[0] // sum(loads)))
    least = 1 if total - largest >= number_of - 1 else 0
    given, surplus = [largest] + [least] * (number_of - 1), total - largest - least * (number_of - 1)
    while surplus > 0:
        movable = [i for i in range(1, number_of) if given[i] < largest] or [i for i in range(1, number_of) if given[i] < reach]
        mass, budget = sum([loads[i] for i in movable]), surplus
        for i in movable:
            more = min(reach - given[i], max(1, budget * loads[i] // mass), surplus)
            given[i] = given[i] + more
            surplus = surplus - more
    return np.array(given)


def setup_inputs(seed: int = 0, part: int = 0) -> dict:
    arg_keys = jax.random.split(jax.random.key(seed), 5)
    part_keys = jax.random.split(jax.random.fold_in(arg_keys[4], part), 5)
    slc = draw_slc(jax.random.fold_in(jax.random.fold_in(arg_keys[4], part), 71), part)
    line_mask = with_ends((jax.random.randint(part_keys[1], (N_ACQ, ROWS), 0, 5) < 4).astype(jnp.int32), jax.random.fold_in(part_keys[1], 1), 0, 1)
    pair_dev_keys = jax.random.split(jax.random.fold_in(arg_keys[2], 1), PAIRS // PAIR_DEV)
    pair_dev_turns = jax.random.permutation(jax.random.fold_in(arg_keys[2], 3), PAIRS // PAIR_DEV)
    pair_dev = jax.vmap(lambda own, number: routed_block(jax.random.fold_in(arg_keys[2], 2), own, number, PAIR_DEV, DATE_DEVS, 2, CAP, 2))(pair_dev_keys, pair_dev_turns).reshape((PAIRS, 2))
    pair_slot = with_ends(jax.random.randint(arg_keys[3], (PAIRS, 2), 0, ACQ_DEV), jax.random.fold_in(arg_keys[3], 1), 0, ACQ_DEV - 1).astype(jnp.int32)
    return dict(slc=slc, line_mask=line_mask, pair_dev=pair_dev, pair_slot=pair_slot)


DAMPING = 0.5
EPSILON = 1e-06

def multilook(field):
    lead = [(0, 0)] * (field.ndim - 2)
    padded = jnp.pad(field, lead + [(1, 1), (4, 4)])
    row_sums = padded[..., 0:-2, :] + padded[..., 1:-1, :] + padded[..., 2:, :]
    width = field.shape[-1]
    total = row_sums[..., :, 0:width]
    for offset in range(1, 9):
        total = total + row_sums[..., :, offset:offset + width]
    return total

def coherence(first, second):
    ref_real = first[:, 0].astype(jnp.float32)
    ref_imag = first[:, 1].astype(jnp.float32)
    sec_real = second[:, 0].astype(jnp.float32)
    sec_imag = second[:, 1].astype(jnp.float32)
    inter_real = ref_real * sec_real + ref_imag * sec_imag
    inter_imag = ref_imag * sec_real - ref_real * sec_imag
    power_ref = ref_real * ref_real + ref_imag * ref_imag
    power_sec = sec_real * sec_real + sec_imag * sec_imag
    scale = jnp.sqrt(jnp.maximum(multilook(power_ref) * multilook(power_sec), 1.0))
    coh_real = multilook(inter_real) / scale
    coh_imag = multilook(inter_imag) / scale
    return (coh_real * coh_real + coh_imag * coh_imag, coh_imag)

def reference(slc, line_mask, pair_dev, pair_slot):
    masked = slc * line_mask[:, None, :, None].astype(jnp.bfloat16)
    end_dates = (pair_dev * ACQ_DEV + pair_slot).astype(jnp.int32)
    first = end_dates[:, 0]
    second = end_dates[:, 1]
    weight, observed = coherence(masked[first], masked[second])
    weighted = weight * observed
    zeros = jnp.zeros((slc.shape[0], slc.shape[2], slc.shape[3]), jnp.float32)
    diagonal = DAMPING + zeros.at[first].add(weight).at[second].add(weight)
    right_side = zeros.at[second].add(weighted).at[first].add(-weighted)

    def operator(vector):
        coupled = zeros.at[first].add(weight * vector[second]).at[second].add(weight * vector[first])
        return diagonal * vector - coupled
    solution = zeros
    residual = right_side
    direction = right_side
    norm_now = lax.optimization_barrier(jnp.sum(residual * residual, axis=0))
    for step in range(ITERS):
        image = operator(direction)
        step_size = norm_now / (lax.optimization_barrier(jnp.sum(direction * image, axis=0)) + EPSILON)
        solution = solution + step_size * direction
        residual = residual - step_size * image
        if step + 1 < ITERS:
            norm_next = lax.optimization_barrier(jnp.sum(residual * residual, axis=0))
            direction = residual + norm_next / (norm_now + EPSILON) * direction
            norm_now = norm_next
    return (solution, residual)
```

```python
import functools

import jax
import jax.numpy as jnp
from jax import lax
from jax.experimental import pallas as pl
from jax.experimental.pallas import tpu as pltpu
from jax.sharding import PartitionSpec as P

ITERS = 2
DAMPING = 0.5
EPSILON = 1e-06
LANES = 128
HALO = 4
F32 = jnp.float32
BF16 = jnp.bfloat16


def iota(shape, dim):
    return lax.broadcasted_iota(jnp.int32, shape, dim)


def dot(a, b):
    return lax.dot_general(a, b, (((1,), (0,)), ((), ())), preferred_element_type=F32)


def split(x):
    high = x.astype(BF16)
    return high, (x - high.astype(F32)).astype(BF16)


def pack_kernel(mask_ref, dev_ref, slot_ref, slc_ref, out_ref):
    parts = out_ref.shape[0]
    dates, _, rows, cols = slc_ref.shape
    width = cols // parts
    blocks = LANES // width
    tiles = slc_ref[...].astype(F32).reshape(dates * 2 * rows, cols).astype(BF16)
    mask = jnp.concatenate(
        [mask_ref[...].astype(F32), jnp.zeros((8 - dates, rows), F32)], axis=0
    )
    lane = iota((8, dates * 2 * rows), 1)
    row = iota((8, dates * 2 * rows), 0)
    picks = []
    for i in range(rows):
        for c in range(2):
            picks.append(jnp.where(lane == (row * 2 + c) * rows + i, mask[:, i : i + 1], 0.0))
    pick = jnp.concatenate(picks, axis=0).astype(BF16)
    lines = dot(pick, tiles)
    place = iota((cols, 8 * parts), 1)
    j = place % 8
    column = (place // 8) * width + jnp.where(j < HALO, j - HALO, width + j - HALO)
    side = (iota((cols, 8 * parts), 0) == column).astype(F32).astype(BF16)
    edges = dot(lines.astype(BF16), side)

    lane = iota((8, LANES), 1)
    row = iota((8, LANES), 0)
    block = lane // width
    block8 = lane // 8
    pair_count = dev_ref.shape[0]
    pair_lane = iota((pair_count, LANES), 1)
    pair_row = iota((pair_count, LANES), 0)

    def along_lanes(ref):
        value = ref[...].astype(F32)
        total = jnp.zeros((1, LANES), F32)
        for t in range(2):
            hit = pair_lane == pair_row + 64 * t
            total = total + jnp.sum(jnp.where(hit, value[:, t : t + 1], 0.0), axis=0, keepdims=True)
        return total

    index_rows = jnp.where(
        row == 6, along_lanes(dev_ref), jnp.where(row == 7, along_lanes(slot_ref), 0.0)
    )

    def rolled(array, i, c, tile, shift):
        at = (i * 2 + c) * 8
        part = array[at : at + 8, tile * LANES : (tile + 1) * LANES]
        return part if shift % LANES == 0 else pltpu.roll(part, shift % LANES, 1)

    for tile in range(cols // LANES):
        main = {
            (c, h, k): rolled(lines, 4 * h + k, c, tile, width * k)
            for c in range(2)
            for h in range(2)
            for k in range(4)
        }
        for q in range(blocks):
            e = tile * blocks + q
            groups = []
            for c in range(2):
                for h in range(2):
                    total = jnp.zeros((8, LANES), F32)
                    for k in range(4):
                        total = jnp.where(block == (q + k) % blocks, main[c, h, k], total)
                    groups.append(total)
            halo = jnp.zeros((8, LANES), F32)
            for i in range(rows):
                for c in range(2):
                    moved = rolled(edges, i, c, e // 16, 8 * (i + 8 * c))
                    halo = jnp.where(block8 == (e + i + 8 * c) % 16, moved, halo)
            for g in range(3):
                groups[g] = jnp.where(row >= 6, pltpu.roll(halo, 6 - 2 * g, 0), groups[g])
            groups[3] = jnp.where(row >= 6, index_rows, groups[3])
            out_ref[e] = jnp.concatenate(groups, axis=0).astype(BF16)


def strip_kernel(
    dates, pair_count, width, chunk, got_ref, out_ref, first_ref, second_ref, diff_ref, diff_t_ref, weight_ref, term_ref
):
    parts = got_ref.shape[0]
    slots = 8 * parts
    blocks = LANES // width
    pairs = parts * pair_count
    me = lax.axis_index("date")

    got = got_ref[...].astype(F32)
    group = [got[:, 8 * g : 8 * g + 8, :] for g in range(4)]
    row = iota((parts, 8, LANES), 1)
    halo = jnp.where(
        row < 2,
        pltpu.roll(group[0], 2, 1),
        jnp.where(row < 4, pltpu.roll(group[1], 4, 1), pltpu.roll(group[2], 6, 1)),
    )
    columns = [x.reshape(slots, LANES) for x in group + [halo]]
    columns.append(pltpu.roll(columns[4], 64, 1))
    tiles = jnp.concatenate([x.astype(BF16) for x in columns], axis=1)

    at = iota((parts, slots), 1) - 8 * iota((parts, slots), 0)
    take = jnp.where(at == 6, 8.0, jnp.where(at == 7, 1.0, 0.0)).astype(BF16)
    ends = dot(take, columns[3].astype(BF16)).astype(jnp.int32)
    lane = iota((parts, slots), 1)
    for k in range(pair_count):
        first = (ends[:, k : k + 1] == lane).astype(F32)
        second = (ends[:, 64 + k : 65 + k] == lane).astype(F32)
        at = pl.ds(k * parts, parts)
        first_ref[at, :] = first.astype(BF16)
        second_ref[at, :] = second.astype(BF16)
        diff = (second - first).astype(BF16)
        diff_ref[at, :] = jnp.concatenate([diff, diff], axis=1)
    diff_t = jnp.transpose(diff_ref[:, 0:slots].astype(F32)).astype(BF16)
    diff_t_ref[...] = jnp.concatenate([diff_t, diff_t], axis=1)

    def main_place(shape, dim):
        p = iota(shape, dim)
        lane = p % LANES
        k = (lane // width - me + 64) % blocks
        line = jnp.where(k < 4, (p // LANES) * 4 + k, 1000 * (dim + 1))
        return line, lane % width

    def halo_place(shape, dim):
        p = iota(shape, dim)
        t = (p // 8 - me + 64) % 16
        j = p % 8
        return t % 8, jnp.where(j < HALO, j - HALO, width + j - HALO), t // 8

    to_line, to_col = main_place((1, 2 * LANES), 1)
    line, col = main_place((2 * LANES, 1), 0)

    def near(line, col):
        hit = (jnp.abs(line - to_line) <= 1) & (jnp.abs(col - to_col) <= HALO)
        return hit.astype(F32)

    band = near(line, col).astype(BF16)
    line, col, imag = halo_place((LANES, 1), 0)
    band_halo = near(line, col)
    band_cross = (band_halo * (2.0 * imag.astype(F32) - 1.0)).astype(BF16)
    band_halo = band_halo.astype(BF16)
    band_halo = jnp.concatenate([band_halo, band_halo], axis=0)
    band_cross = jnp.concatenate([band_cross, band_cross], axis=0)

    def looks(field, edge, edge_band):
        high, low = split(field)
        edge_high, edge_low = split(edge)
        edges = jnp.concatenate([edge_high, edge_low], axis=1)
        return dot(high, band) + dot(low, band) + dot(edges, edge_band)

    def body(step, carry):
        at = pl.ds(pl.multiple_of(step * chunk, chunk), chunk)
        u = dot(first_ref[at, :], tiles)
        v = dot(second_ref[at, :], tiles)
        u_re, u_im, u_halo = u[:, 0:256], u[:, 256:512], u[:, 512:640]
        v_re, v_im, v_halo, v_swap = v[:, 0:256], v[:, 256:512], v[:, 512:640], v[:, 640:768]
        real = looks(u_re * v_re + u_im * v_im, u_halo * v_halo, band_halo)
        imag = looks(u_im * v_re - u_re * v_im, u_halo * v_swap, band_cross)
        power_ref = looks(u_re * u_re + u_im * u_im, u_halo * u_halo, band_halo)
        power_sec = looks(v_re * v_re + v_im * v_im, v_halo * v_halo, band_halo)
        scale = lax.rsqrt(jnp.maximum(power_ref * power_sec, 1.0))
        real = real * scale
        imag = imag * scale
        weight = real * real + imag * imag
        weight_ref[at, :] = weight
        high, low = split(weight * imag)
        term_ref[at, :] = high
        term_ref[pl.ds(pl.multiple_of(pairs + step * chunk, 16), chunk), :] = low
        return carry

    lax.fori_loop(0, pairs // chunk, body, 0)

    right_side = dot(diff_t_ref[...], term_ref[...])

    def operator(field):
        high, low = split(field)
        spread = dot(diff_ref[...], jnp.concatenate([high, low], axis=0))
        high, low = split(weight_ref[...] * spread)
        term_ref[0:pairs, :] = high
        term_ref[pairs : 2 * pairs, :] = low
        return DAMPING * field + dot(diff_t_ref[...], term_ref[...])

    def inner(a, b):
        return jnp.sum(a * b, axis=0, keepdims=True)

    solution = jnp.zeros_like(right_side)
    residual = right_side
    direction = right_side
    norm_now = inner(residual, residual)
    for step in range(ITERS):
        image = operator(direction)
        step_size = norm_now / (inner(direction, image) + EPSILON)
        solution = solution + step_size * direction
        residual = residual - step_size * image
        if step + 1 < ITERS:
            norm_next = inner(residual, residual)
            direction = residual + norm_next / (norm_now + EPSILON) * direction
            norm_now = norm_next
    for o, field in enumerate((solution, residual)):
        field = field.reshape(parts, 8, 2 * LANES)
        for h in range(2):
            at = (2 * o + h) * dates
            out_ref[:, at : at + dates, :] = field[:, 0:dates, h * LANES : (h + 1) * LANES]


def unpack_kernel(got_ref, *out_refs):
    parts = got_ref.shape[0]
    dates, rows, cols = out_refs[0].shape
    width = cols // parts
    blocks = LANES // width
    block = iota((dates, LANES), 1) // width
    for o, out_ref in enumerate(out_refs):
        for h in range(2):
            at = (2 * o + h) * dates
            for tile in range(cols // LANES):
                for k in range(4):
                    total = jnp.zeros((dates, LANES), F32)
                    for q in range(blocks):
                        part = got_ref[tile * blocks + q, at : at + dates, :]
                        total = jnp.where(block == (q + k) % blocks, part, total)
                    shift = -width * k % LANES
                    if shift:
                        total = pltpu.roll(total, shift, 1)
                    out_ref[:, 4 * h + k, tile * LANES : (tile + 1) * LANES] = total


def shards(slc, line_mask, pair_dev, pair_slot):
    parts = lax.axis_size("date")
    dates, _, rows, cols = slc.shape
    pair_count = pair_dev.shape[0]
    pairs = parts * pair_count
    width = cols // parts
    chunk = max(c for c in range(16, 129, 16) if pairs % c == 0)
    vmem = pl.BlockSpec(memory_space=pltpu.VMEM)

    packed = pl.pallas_call(
        pack_kernel,
        out_shape=jax.ShapeDtypeStruct((parts, 32, LANES), BF16),
        in_specs=[vmem] * 4,
        out_specs=vmem,
        name="pack",
    )(line_mask, pair_dev, pair_slot, slc)
    got = lax.all_to_all(packed, "date", split_axis=0, concat_axis=0, tiled=True)
    fields = pl.pallas_call(
        functools.partial(strip_kernel, dates, pair_count, width, chunk),
        out_shape=jax.ShapeDtypeStruct((parts, 4 * dates, LANES), F32),
        in_specs=[vmem],
        out_specs=vmem,
        scratch_shapes=[
            pltpu.VMEM((pairs, 8 * parts), BF16),
            pltpu.VMEM((pairs, 8 * parts), BF16),
            pltpu.VMEM((pairs, 16 * parts), BF16),
            pltpu.VMEM((8 * parts, 2 * pairs), BF16),
            pltpu.VMEM((pairs, 2 * LANES), F32),
            pltpu.VMEM((2 * pairs, 2 * LANES), BF16),
        ],
        compiler_params=pltpu.CompilerParams(vmem_limit_bytes=48 * 1024 * 1024),
        name="strip",
    )(got)
    back = lax.all_to_all(fields, "date", split_axis=0, concat_axis=0, tiled=True)
    out = jax.ShapeDtypeStruct((dates, rows, cols), F32)
    return pl.pallas_call(
        unpack_kernel,
        out_shape=(out, out),
        in_specs=[vmem],
        out_specs=(vmem, vmem),
        name="unpack",
    )(back)


def solution(mesh):
    in_specs = (P("date", None, "grp", None), P("date", "grp"), P("date", None), P("date", None))
    out_specs = (P("date", "grp", None), P("date", "grp", None))
    return jax.shard_map(shards, mesh=mesh, in_specs=in_specs, out_specs=out_specs, check_vma=False)
```

```python
import functools

import jax
import jax.numpy as jnp
from jax import lax
from jax.experimental import pallas as pl
from jax.experimental.pallas import tpu as pltpu
from jax.sharding import PartitionSpec as P

ITERS = 2
DAMPING = 0.5
EPSILON = 1e-06
LANES = 128
HALO = 4
F32 = jnp.float32
BF16 = jnp.bfloat16


def iota(shape, dim):
    return lax.broadcasted_iota(jnp.int32, shape, dim)


def dot(a, b):
    return lax.dot_general(a, b, (((1,), (0,)), ((), ())), preferred_element_type=F32)


def split(x):
    high = x.astype(BF16)
    return high, (x - high.astype(F32)).astype(BF16)


def pack_kernel(mask_ref, dev_ref, slot_ref, slc_ref, out_ref):
    parts = out_ref.shape[0]
    dates, _, rows, cols = slc_ref.shape
    width = cols // parts
    blocks = LANES // width
    tiles = slc_ref[...].astype(F32).reshape(dates * 2 * rows, cols).astype(BF16)
    mask = jnp.concatenate(
        [mask_ref[...].astype(F32), jnp.zeros((8 - dates, rows), F32)], axis=0
    )
    lane = iota((8, dates * 2 * rows), 1)
    row = iota((8, dates * 2 * rows), 0)
    picks = []
    for i in range(rows):
        for c in range(2):
            picks.append(jnp.where(lane == (row * 2 + c) * rows + i, mask[:, i : i + 1], 0.0))
    pick = jnp.concatenate(picks, axis=0).astype(BF16)
    lines = dot(pick, tiles)
    place = iota((cols, 8 * parts), 1)
    j = place % 8
    column = (place // 8) * width + jnp.where(j < HALO, j - HALO, width + j - HALO)
    side = (iota((cols, 8 * parts), 0) == column).astype(F32).astype(BF16)
    edges = dot(lines.astype(BF16), side)

    lane = iota((8, LANES), 1)
    row = iota((8, LANES), 0)
    block = lane // width
    block8 = lane // 8
    pair_count = dev_ref.shape[1]
    spare = jnp.zeros((2, 64 - pair_count), F32)
    index_rows = jnp.concatenate(
        [dev_ref[...].astype(F32), spare, slot_ref[...].astype(F32), spare], axis=1
    )
    index_rows = jnp.concatenate([jnp.zeros((6, LANES), F32), index_rows], axis=0)

    def rolled(array, i, c, tile, shift):
        at = (i * 2 + c) * 8
        part = array[at : at + 8, tile * LANES : (tile + 1) * LANES]
        return part if shift % LANES == 0 else pltpu.roll(part, shift % LANES, 1)

    for tile in range(cols // LANES):
        main = {
            (c, h, k): rolled(lines, 4 * h + k, c, tile, width * k)
            for c in range(2)
            for h in range(2)
            for k in range(4)
        }
        for q in range(blocks):
            e = tile * blocks + q
            groups = []
            for c in range(2):
                for h in range(2):
                    total = jnp.zeros((8, LANES), F32)
                    for k in range(4):
                        total = jnp.where(block == (q + k) % blocks, main[c, h, k], total)
                    groups.append(total)
            halo = jnp.zeros((8, LANES), F32)
            for i in range(rows):
                for c in range(2):
                    moved = rolled(edges, i, c, e // 16, 8 * (i + 8 * c))
                    halo = jnp.where(block8 == (e + i + 8 * c) % 16, moved, halo)
            for g in range(3):
                groups[g] = jnp.where(row >= 6, pltpu.roll(halo, 6 - 2 * g, 0), groups[g])
            groups[3] = jnp.where(row >= 6, index_rows, groups[3])
            out_ref[e] = jnp.concatenate(groups, axis=0).astype(BF16)


def strip_kernel(
    dates, pair_count, width, chunk, got_ref, out_ref, first_ref, second_ref, diff_ref, diff_t_ref, weight_ref, term_ref
):
    parts = got_ref.shape[0]
    slots = 8 * parts
    blocks = LANES // width
    pairs = parts * pair_count
    me = lax.axis_index("date")

    got = got_ref[...].astype(F32)
    group = [got[:, 8 * g : 8 * g + 8, :] for g in range(4)]
    row = iota((parts, 8, LANES), 1)
    halo = jnp.where(
        row < 2,
        pltpu.roll(group[0], 2, 1),
        jnp.where(row < 4, pltpu.roll(group[1], 4, 1), pltpu.roll(group[2], 6, 1)),
    )
    columns = [x.reshape(slots, LANES) for x in group + [halo]]
    columns.append(pltpu.roll(columns[4], 64, 1))
    tiles = jnp.concatenate([x.astype(BF16) for x in columns], axis=1)

    at = iota((2 * parts, slots), 1) - 8 * (iota((2 * parts, slots), 0) % parts)
    take = (at == 6 + iota((2 * parts, slots), 0) // parts).astype(F32).astype(BF16)
    ends = dot(take, columns[3].astype(BF16))
    ends = (8.0 * ends + pltpu.roll(ends, 64, 1)).astype(jnp.int32)
    lane = iota((parts, slots), 1)
    for k in range(pair_count):
        first = (ends[0:parts, k : k + 1] == lane).astype(F32)
        second = (ends[parts : 2 * parts, k : k + 1] == lane).astype(F32)
        at = pl.ds(k * parts, parts)
        first_ref[at, :] = first.astype(BF16)
        second_ref[at, :] = second.astype(BF16)
        diff = (second - first).astype(BF16)
        diff_ref[at, :] = jnp.concatenate([diff, diff], axis=1)
    diff_t = jnp.transpose(diff_ref[:, 0:slots].astype(F32)).astype(BF16)
    diff_t_ref[...] = jnp.concatenate([diff_t, diff_t], axis=1)

    def main_place(shape, dim):
        p = iota(shape, dim)
        lane = p % LANES
        k = (lane // width - me + 64) % blocks
        line = jnp.where(k < 4, (p // LANES) * 4 + k, 1000 * (dim + 1))
        return line, lane % width

    def halo_place(shape, dim):
        p = iota(shape, dim)
        t = (p // 8 - me + 64) % 16
        j = p % 8
        return t % 8, jnp.where(j < HALO, j - HALO, width + j - HALO), t // 8

    to_line, to_col = main_place((1, 2 * LANES), 1)
    line, col = main_place((2 * LANES, 1), 0)

    def near(line, col):
        hit = (jnp.abs(line - to_line) <= 1) & (jnp.abs(col - to_col) <= HALO)
        return hit.astype(F32)

    band = near(line, col).astype(BF16)
    line, col, imag = halo_place((LANES, 1), 0)
    band_halo = near(line, col)
    band_cross = (band_halo * (2.0 * imag.astype(F32) - 1.0)).astype(BF16)
    band_halo = band_halo.astype(BF16)
    band_halo = jnp.concatenate([band_halo, band_halo], axis=0)
    band_cross = jnp.concatenate([band_cross, band_cross], axis=0)

    def looks(field, edge, edge_band):
        high, low = split(field)
        edge_high, edge_low = split(edge)
        edges = jnp.concatenate([edge_high, edge_low], axis=1)
        return dot(high, band) + dot(low, band) + dot(edges, edge_band)

    def body(step, carry):
        at = pl.ds(pl.multiple_of(step * chunk, chunk), chunk)
        u = dot(first_ref[at, :], tiles)
        v = dot(second_ref[at, :], tiles)
        u_re, u_im, u_halo = u[:, 0:256], u[:, 256:512], u[:, 512:640]
        v_re, v_im, v_halo, v_swap = v[:, 0:256], v[:, 256:512], v[:, 512:640], v[:, 640:768]
        real = looks(u_re * v_re + u_im * v_im, u_halo * v_halo, band_halo)
        imag = looks(u_im * v_re - u_re * v_im, u_halo * v_swap, band_cross)
        power_ref = looks(u_re * u_re + u_im * u_im, u_halo * u_halo, band_halo)
        power_sec = looks(v_re * v_re + v_im * v_im, v_halo * v_halo, band_halo)
        scale = lax.rsqrt(jnp.maximum(power_ref * power_sec, 1.0))
        real = real * scale
        imag = imag * scale
        weight = real * real + imag * imag
        weight_ref[at, :] = weight
        high, low = split(weight * imag)
        term_ref[at, :] = high
        term_ref[pl.ds(pl.multiple_of(pairs + step * chunk, 16), chunk), :] = low
        return carry

    lax.fori_loop(0, pairs // chunk, body, 0)

    right_side = dot(diff_t_ref[...], term_ref[...])

    def operator(field):
        high, low = split(field)
        spread = dot(diff_ref[...], jnp.concatenate([high, low], axis=0))
        high, low = split(weight_ref[...] * spread)
        term_ref[0:pairs, :] = high
        term_ref[pairs : 2 * pairs, :] = low
        return DAMPING * field + dot(diff_t_ref[...], term_ref[...])

    def inner(a, b):
        return jnp.sum(a * b, axis=0, keepdims=True)

    solution = jnp.zeros_like(right_side)
    residual = right_side
    direction = right_side
    norm_now = inner(residual, residual)
    for step in range(ITERS):
        image = operator(direction)
        step_size = norm_now / (inner(direction, image) + EPSILON)
        solution = solution + step_size * direction
        residual = residual - step_size * image
        if step + 1 < ITERS:
            norm_next = inner(residual, residual)
            direction = residual + norm_next / (norm_now + EPSILON) * direction
            norm_now = norm_next
    for o, field in enumerate((solution, residual)):
        field = field.reshape(parts, 8, 2 * LANES)
        for h in range(2):
            at = (2 * o + h) * dates
            out_ref[:, at : at + dates, :] = field[:, 0:dates, h * LANES : (h + 1) * LANES]


def unpack_kernel(got_ref, *out_refs):
    parts = got_ref.shape[0]
    dates, rows, cols = out_refs[0].shape
    width = cols // parts
    blocks = LANES // width
    block = iota((dates, LANES), 1) // width
    for o, out_ref in enumerate(out_refs):
        for h in range(2):
            at = (2 * o + h) * dates
            for tile in range(cols // LANES):
                for k in range(4):
                    total = jnp.zeros((dates, LANES), F32)
                    for q in range(blocks):
                        part = got_ref[tile * blocks + q, at : at + dates, :]
                        total = jnp.where(block == (q + k) % blocks, part, total)
                    shift = -width * k % LANES
                    if shift:
                        total = pltpu.roll(total, shift, 1)
                    out_ref[:, 4 * h + k, tile * LANES : (tile + 1) * LANES] = total


def shards(slc, line_mask, pair_dev, pair_slot):
    parts = lax.axis_size("date")
    dates, _, rows, cols = slc.shape
    pair_count = pair_dev.shape[0]
    pairs = parts * pair_count
    width = cols // parts
    chunk = max(c for c in range(16, 129, 16) if pairs % c == 0)
    vmem = pl.BlockSpec(memory_space=pltpu.VMEM)

    packed = pl.pallas_call(
        pack_kernel,
        out_shape=jax.ShapeDtypeStruct((parts, 32, LANES), BF16),
        in_specs=[vmem] * 4,
        out_specs=vmem,
        compiler_params=pltpu.CompilerParams(vmem_limit_bytes=4 * 1024 * 1024),
        name="pack",
    )(line_mask, pair_dev.T, pair_slot.T, slc)
    got = lax.all_to_all(packed, "date", split_axis=0, concat_axis=0, tiled=True)
    fields = pl.pallas_call(
        functools.partial(strip_kernel, dates, pair_count, width, chunk),
        out_shape=jax.ShapeDtypeStruct((parts, 4 * dates, LANES), F32),
        in_specs=[vmem],
        out_specs=vmem,
        scratch_shapes=[
            pltpu.VMEM((pairs, 8 * parts), BF16),
            pltpu.VMEM((pairs, 8 * parts), BF16),
            pltpu.VMEM((pairs, 16 * parts), BF16),
            pltpu.VMEM((8 * parts, 2 * pairs), BF16),
            pltpu.VMEM((pairs, 2 * LANES), F32),
            pltpu.VMEM((2 * pairs, 2 * LANES), BF16),
        ],
        compiler_params=pltpu.CompilerParams(vmem_limit_bytes=24 * 1024 * 1024),
        name="strip",
    )(got)
    back = lax.all_to_all(fields, "date", split_axis=0, concat_axis=0, tiled=True)
    out = jax.ShapeDtypeStruct((dates, rows, cols), F32)
    return pl.pallas_call(
        unpack_kernel,
        out_shape=(out, out),
        in_specs=[vmem],
        out_specs=(vmem, vmem),
        compiler_params=pltpu.CompilerParams(vmem_limit_bytes=4 * 1024 * 1024),
        name="unpack",
    )(back)


def solution(mesh):
    in_specs = (P("date", None, "grp", None), P("date", "grp"), P("date", None), P("date", None))
    out_specs = (P("date", "grp", None), P("date", "grp", None))
    return jax.shard_map(shards, mesh=mesh, in_specs=in_specs, out_specs=out_specs, check_vma=False)
```

```python
import functools

import jax
import jax.numpy as jnp
from jax import lax
from jax.experimental import pallas as pl
from jax.experimental.pallas import tpu as pltpu
from jax.sharding import PartitionSpec as P

ITERS = 2
DAMPING = 0.5
EPSILON = 1e-06
LANES = 128
HALO = 4
F32 = jnp.float32
BF16 = jnp.bfloat16


def iota(shape, dim):
    return lax.broadcasted_iota(jnp.int32, shape, dim)


def dot(a, b):
    return lax.dot_general(a, b, (((1,), (0,)), ((), ())), preferred_element_type=F32)


def split(x):
    high = x.astype(BF16)
    return high, (x - high.astype(F32)).astype(BF16)


def pack_kernel(mask_in, dev_in, slot_in, slc_in, out_ref, mask_ref, dev_ref, slot_ref, slc_ref, sems):
    copies = [
        pltpu.make_async_copy(source, target, sems.at[n])
        for n, (source, target) in enumerate(
            ((slc_in, slc_ref), (mask_in, mask_ref), (dev_in, dev_ref), (slot_in, slot_ref))
        )
    ]
    for copy in copies:
        copy.start()
    for copy in copies:
        copy.wait()
    parts = out_ref.shape[0]
    dates, _, rows, cols = slc_ref.shape
    width = cols // parts
    blocks = LANES // width
    tiles = slc_ref[...].astype(F32).reshape(dates * 2 * rows, cols).astype(BF16)
    mask = jnp.concatenate(
        [mask_ref[...].astype(F32), jnp.zeros((8 - dates, rows), F32)], axis=0
    )
    lane = iota((8, dates * 2 * rows), 1)
    row = iota((8, dates * 2 * rows), 0)
    picks = []
    for i in range(rows):
        for c in range(2):
            picks.append(jnp.where(lane == (row * 2 + c) * rows + i, mask[:, i : i + 1], 0.0))
    pick = jnp.concatenate(picks, axis=0).astype(BF16)
    lines = dot(pick, tiles)
    place = iota((cols, 8 * parts), 1)
    j = place % 8
    column = (place // 8) * width + jnp.where(j < HALO, j - HALO, width + j - HALO)
    side = (iota((cols, 8 * parts), 0) == column).astype(F32).astype(BF16)
    edges = dot(lines.astype(BF16), side)

    lane = iota((8, LANES), 1)
    row = iota((8, LANES), 0)
    block = lane // width
    block8 = lane // 8
    pair_count = dev_ref.shape[1]
    spare = jnp.zeros((2, 64 - pair_count), F32)
    index_rows = jnp.concatenate(
        [dev_ref[...].astype(F32), spare, slot_ref[...].astype(F32), spare], axis=1
    )
    index_rows = jnp.concatenate([jnp.zeros((6, LANES), F32), index_rows], axis=0)

    def rolled(array, i, c, tile, shift):
        at = (i * 2 + c) * 8
        part = array[at : at + 8, tile * LANES : (tile + 1) * LANES]
        return part if shift % LANES == 0 else pltpu.roll(part, shift % LANES, 1)

    for tile in range(cols // LANES):
        main = {
            (c, h, k): rolled(lines, 4 * h + k, c, tile, width * k)
            for c in range(2)
            for h in range(2)
            for k in range(4)
        }
        for q in range(blocks):
            e = tile * blocks + q
            groups = []
            for c in range(2):
                for h in range(2):
                    total = jnp.zeros((8, LANES), F32)
                    for k in range(4):
                        total = jnp.where(block == (q + k) % blocks, main[c, h, k], total)
                    groups.append(total)
            halo = jnp.zeros((8, LANES), F32)
            for i in range(rows):
                for c in range(2):
                    moved = rolled(edges, i, c, e // 16, 8 * (i + 8 * c))
                    halo = jnp.where(block8 == (e + i + 8 * c) % 16, moved, halo)
            for g in range(3):
                groups[g] = jnp.where(row >= 6, pltpu.roll(halo, 6 - 2 * g, 0), groups[g])
            groups[3] = jnp.where(row >= 6, index_rows, groups[3])
            out_ref[e] = jnp.concatenate(groups, axis=0).astype(BF16)


def strip_kernel(
    dates, pair_count, width, chunk, got_ref, out_ref, first_ref, second_ref, diff_ref, diff_t_ref, weight_ref, term_ref
):
    parts = got_ref.shape[0]
    slots = 8 * parts
    blocks = LANES // width
    pairs = parts * pair_count
    me = lax.axis_index("date")

    got = got_ref[...].astype(F32)
    group = [got[:, 8 * g : 8 * g + 8, :] for g in range(4)]
    row = iota((parts, 8, LANES), 1)
    halo = jnp.where(
        row < 2,
        pltpu.roll(group[0], 2, 1),
        jnp.where(row < 4, pltpu.roll(group[1], 4, 1), pltpu.roll(group[2], 6, 1)),
    )
    columns = [x.reshape(slots, LANES) for x in group + [halo]]

    at = iota((2 * parts, slots), 1) - 8 * (iota((2 * parts, slots), 0) % parts)
    take = (at == 6 + iota((2 * parts, slots), 0) // parts).astype(F32).astype(BF16)
    ends = dot(take, columns[3].astype(BF16))
    ends = (8.0 * ends + pltpu.roll(ends, 64, 1)).astype(jnp.int32)
    lane = iota((parts, slots), 1)
    for k in range(pair_count):
        first = (ends[0:parts, k : k + 1] == lane).astype(F32)
        second = (ends[parts : 2 * parts, k : k + 1] == lane).astype(F32)
        at = pl.ds(k * parts, parts)
        for ref, value in ((first_ref, first), (second_ref, second), (diff_ref, second - first)):
            value = value.astype(BF16)
            ref[at, :] = jnp.concatenate([value, value], axis=1)
    diff_t = jnp.transpose(diff_ref[:, 0:slots].astype(F32)).astype(BF16)
    diff_t_ref[...] = jnp.concatenate([diff_t, diff_t], axis=1)

    def main_place(shape, dim):
        p = iota(shape, dim)
        lane = p % LANES
        k = (lane // width - me + 64) % blocks
        line = jnp.where(k < 4, (p // LANES) * 4 + k, 1000 * (dim + 1))
        return line, lane % width

    def halo_place(shape, dim):
        p = iota(shape, dim)
        t = (p // 8 - me + 64) % 16
        j = p % 8
        return t % 8, jnp.where(j < HALO, j - HALO, width + j - HALO), t // 8

    to_line, to_col = main_place((1, 2 * LANES), 1)

    def near(line, col):
        hit = (jnp.abs(line - to_line) <= 1) & (jnp.abs(col - to_col) <= HALO)
        return hit.astype(F32)

    band = near(*main_place((2 * LANES, 1), 0)).astype(BF16)
    line, col, imag = halo_place((LANES, 1), 0)
    band_halo = near(line, col)
    band_cross = (band_halo * (2.0 * imag.astype(F32) - 1.0)).astype(BF16)
    band_halo = band_halo.astype(BF16)
    band_halo = jnp.concatenate([band, band, band_halo, band_halo], axis=0)
    band_cross = jnp.concatenate([band, band, band_cross, band_cross], axis=0)

    def looks(field, edge, table):
        return dot(jnp.concatenate([*split(field), *split(edge)], axis=1), table)

    re = jnp.concatenate(columns[0:2], axis=1)
    im = jnp.concatenate(columns[2:4], axis=1)
    power_high, power_low = split(looks(re * re + im * im, columns[4] * columns[4], band_halo))
    tiles = jnp.concatenate([x.astype(BF16) for x in columns], axis=1)
    swap = pltpu.roll(columns[4], 64, 1).astype(BF16)
    zero = jnp.zeros_like(tiles)
    first_tiles = jnp.concatenate(
        [
            jnp.concatenate([power_high, tiles], axis=1),
            jnp.concatenate([power_low, zero], axis=1),
        ],
        axis=0,
    )
    second_tiles = jnp.concatenate(
        [
            jnp.concatenate([power_high, tiles, swap], axis=1),
            jnp.concatenate([power_low, zero, jnp.zeros_like(swap)], axis=1),
        ],
        axis=0,
    )

    def body(step, carry):
        at = pl.ds(pl.multiple_of(step * chunk, 16), chunk)
        u = dot(first_ref[at, :], first_tiles)
        v = dot(second_ref[at, :], second_tiles)
        u_power, u_re, u_im, u_halo = u[:, 0:256], u[:, 256:512], u[:, 512:768], u[:, 768:896]
        v_power, v_re, v_im, v_halo = v[:, 0:256], v[:, 256:512], v[:, 512:768], v[:, 768:896]
        real = looks(u_re * v_re + u_im * v_im, u_halo * v_halo, band_halo)
        imag = looks(u_im * v_re - u_re * v_im, u_halo * v[:, 896:1024], band_cross)
        scale = lax.rsqrt(jnp.maximum(u_power * v_power, 1.0))
        real = real * scale
        imag = imag * scale
        weight = real * real + imag * imag
        weight_ref[at, :] = weight
        high, low = split(weight * imag)
        term_ref[at, :] = high
        term_ref[pl.ds(pl.multiple_of(pairs + step * chunk, 16), chunk), :] = low
        return carry

    if chunk == pairs:
        body(0, 0)
    else:
        lax.fori_loop(0, pairs // chunk, body, 0)

    right_side = dot(diff_t_ref[...], term_ref[...])

    def operator(field):
        high, low = split(field)
        spread = dot(diff_ref[...], jnp.concatenate([high, low], axis=0))
        high, low = split(weight_ref[...] * spread)
        term_ref[0:pairs, :] = high
        term_ref[pairs : 2 * pairs, :] = low
        return DAMPING * field + dot(diff_t_ref[...], term_ref[...])

    def inner(a, b):
        return jnp.sum(a * b, axis=0, keepdims=True)

    solution = jnp.zeros_like(right_side)
    residual = right_side
    direction = right_side
    norm_now = inner(residual, residual)
    for step in range(ITERS):
        image = operator(direction)
        step_size = norm_now / (inner(direction, image) + EPSILON)
        solution = solution + step_size * direction
        residual = residual - step_size * image
        if step + 1 < ITERS:
            norm_next = inner(residual, residual)
            direction = residual + norm_next / (norm_now + EPSILON) * direction
            norm_now = norm_next
    for o, field in enumerate((solution, residual)):
        field = field.reshape(parts, 8, 2 * LANES)
        for h in range(2):
            at = (2 * o + h) * dates
            out_ref[:, at : at + dates, :] = field[:, 0:dates, h * LANES : (h + 1) * LANES]


def unpack_kernel(got_ref, *out_refs):
    parts = got_ref.shape[0]
    dates, rows, cols = out_refs[0].shape
    width = cols // parts
    blocks = LANES // width
    block = iota((dates, LANES), 1) // width
    for o, out_ref in enumerate(out_refs):
        for h in range(2):
            at = (2 * o + h) * dates
            for tile in range(cols // LANES):
                for k in range(4):
                    total = jnp.zeros((dates, LANES), F32)
                    for q in range(blocks):
                        part = got_ref[tile * blocks + q, at : at + dates, :]
                        total = jnp.where(block == (q + k) % blocks, part, total)
                    shift = -width * k % LANES
                    if shift:
                        total = pltpu.roll(total, shift, 1)
                    out_ref[:, 4 * h + k, tile * LANES : (tile + 1) * LANES] = total


def shards(slc, line_mask, pair_dev, pair_slot):
    parts = lax.axis_size("date")
    dates, _, rows, cols = slc.shape
    pair_count = pair_dev.shape[0]
    pairs = parts * pair_count
    width = cols // parts
    chunk = max(c for c in range(16, 513, 16) if pairs % c == 0)
    vmem = pl.BlockSpec(memory_space=pltpu.VMEM)

    packed = pl.pallas_call(
        pack_kernel,
        out_shape=jax.ShapeDtypeStruct((parts, 32, LANES), BF16),
        in_specs=[pl.BlockSpec(memory_space=pltpu.HBM)] * 4,
        out_specs=vmem,
        scratch_shapes=[
            pltpu.VMEM((dates, rows), jnp.int32),
            pltpu.VMEM((2, pair_count), jnp.int32),
            pltpu.VMEM((2, pair_count), jnp.int32),
            pltpu.VMEM(slc.shape, BF16),
            pltpu.SemaphoreType.DMA((4,)),
        ],
        compiler_params=pltpu.CompilerParams(vmem_limit_bytes=4 * 1024 * 1024),
        name="pack",
    )(
        *[
            pltpu.with_memory_space_constraint(x, pltpu.HBM)
            for x in (line_mask, pair_dev.T, pair_slot.T, slc)
        ]
    )
    got = lax.all_to_all(packed, "date", split_axis=0, concat_axis=0, tiled=True)
    fields = pl.pallas_call(
        functools.partial(strip_kernel, dates, pair_count, width, chunk),
        out_shape=jax.ShapeDtypeStruct((parts, 4 * dates, LANES), F32),
        in_specs=[vmem],
        out_specs=vmem,
        scratch_shapes=[
            pltpu.VMEM((pairs, 16 * parts), BF16),
            pltpu.VMEM((pairs, 16 * parts), BF16),
            pltpu.VMEM((pairs, 16 * parts), BF16),
            pltpu.VMEM((8 * parts, 2 * pairs), BF16),
            pltpu.VMEM((pairs, 2 * LANES), F32),
            pltpu.VMEM((2 * pairs, 2 * LANES), BF16),
        ],
        compiler_params=pltpu.CompilerParams(vmem_limit_bytes=24 * 1024 * 1024),
        name="strip",
    )(got)
    back = lax.all_to_all(fields, "date", split_axis=0, concat_axis=0, tiled=True)
    out = jax.ShapeDtypeStruct((dates, rows, cols), F32)
    return pl.pallas_call(
        unpack_kernel,
        out_shape=(out, out),
        in_specs=[vmem],
        out_specs=(vmem, vmem),
        compiler_params=pltpu.CompilerParams(vmem_limit_bytes=4 * 1024 * 1024),
        name="unpack",
    )(back)


def solution(mesh):
    in_specs = (P("date", None, "grp", None), P("date", "grp"), P("date", None), P("date", None))
    out_specs = (P("date", "grp", None), P("date", "grp", None))
    return jax.shard_map(shards, mesh=mesh, in_specs=in_specs, out_specs=out_specs, check_vma=False)
```

```python
import functools

import jax
import jax.numpy as jnp
from jax import lax
from jax.experimental import pallas as pl
from jax.experimental.pallas import tpu as pltpu
from jax.sharding import PartitionSpec as P

ITERS = 2
DAMPING = 0.5
EPSILON = 1e-06
LANES = 128
HALO = 4
F32 = jnp.float32
BF16 = jnp.bfloat16


def iota(shape, dim):
    return lax.broadcasted_iota(jnp.int32, shape, dim)


def dot(a, b):
    return lax.dot_general(a, b, (((1,), (0,)), ((), ())), preferred_element_type=F32)


def split(x):
    high = x.astype(BF16)
    return high, (x - high.astype(F32)).astype(BF16)


def pack_kernel(mask_in, dev_in, slot_in, slc_in, out_ref, mask_ref, dev_ref, slot_ref, slc_ref, side_ref, sems):
    step = slc_ref.shape[0] // 3
    copies = [
        pltpu.make_async_copy(source, target, sems.at[n])
        for n, (source, target) in enumerate(
            [(mask_in, mask_ref), (dev_in, dev_ref), (slot_in, slot_ref)]
            + [
                (slc_in.at[pl.ds(a, step)], slc_ref.at[pl.ds(a, step)])
                for a in range(0, slc_ref.shape[0], step)
            ]
        )
    ]
    for copy in copies:
        copy.start()
    parts = out_ref.shape[0]
    dates, _, rows, cols = slc_ref.shape
    width = cols // parts
    blocks = LANES // width
    place = iota((cols, 8 * parts), 1)
    j = place % 8
    column = (place // 8) * width + jnp.where(j < HALO, j - HALO, width + j - HALO)
    side_ref[...] = (iota((cols, 8 * parts), 0) == column).astype(F32).astype(BF16)
    for copy in copies[:3]:
        copy.wait()
    mask = jnp.concatenate(
        [mask_ref[...].astype(F32), jnp.zeros((8 - dates, rows), F32)], axis=0
    )
    lane = iota((8, dates * 2 * rows), 1)
    row = iota((8, dates * 2 * rows), 0)
    picks = []
    for i in range(rows):
        for c in range(2):
            picks.append(jnp.where(lane == (row * 2 + c) * rows + i, mask[:, i : i + 1], 0.0))
    pick = jnp.concatenate(picks, axis=0).astype(BF16)
    for copy in copies[3:]:
        copy.wait()
    tiles = slc_ref[...].astype(F32).reshape(dates * 2 * rows, cols).astype(BF16)
    lines = dot(pick, tiles)
    edges = dot(lines.astype(BF16), side_ref[...])

    lane = iota((8, LANES), 1)
    row = iota((8, LANES), 0)
    block = lane // width
    block8 = lane // 8
    pair_count = dev_ref.shape[1]
    spare = jnp.zeros((2, 64 - pair_count), F32)
    index_rows = jnp.concatenate(
        [dev_ref[...].astype(F32), spare, slot_ref[...].astype(F32), spare], axis=1
    )
    index_rows = jnp.concatenate([jnp.zeros((6, LANES), F32), index_rows], axis=0)

    def rolled(array, i, c, tile, shift):
        at = (i * 2 + c) * 8
        part = array[at : at + 8, tile * LANES : (tile + 1) * LANES]
        return part if shift % LANES == 0 else pltpu.roll(part, shift % LANES, 1)

    for tile in range(cols // LANES):
        main = {
            (c, h, k): rolled(lines, 4 * h + k, c, tile, width * k)
            for c in range(2)
            for h in range(2)
            for k in range(4)
        }
        for q in range(blocks):
            e = tile * blocks + q
            groups = []
            for c in range(2):
                for h in range(2):
                    total = jnp.zeros((8, LANES), F32)
                    for k in range(4):
                        total = jnp.where(block == (q + k) % blocks, main[c, h, k], total)
                    groups.append(total)
            halo = jnp.zeros((8, LANES), F32)
            for i in range(rows):
                for c in range(2):
                    moved = rolled(edges, i, c, e // 16, 8 * (i + 8 * c))
                    halo = jnp.where(block8 == (e + i + 8 * c) % 16, moved, halo)
            for g in range(3):
                groups[g] = jnp.where(row >= 6, pltpu.roll(halo, 6 - 2 * g, 0), groups[g])
            groups[3] = jnp.where(row >= 6, index_rows, groups[3])
            out_ref[e] = jnp.concatenate(groups, axis=0).astype(BF16)


def strip_kernel(
    dates, pair_count, width, chunk, got_ref, out_ref, first_ref, second_ref, diff_ref, diff_t_ref, weight_ref, term_ref
):
    parts = got_ref.shape[0]
    slots = 8 * parts
    blocks = LANES // width
    pairs = parts * pair_count
    me = lax.axis_index("date")

    got = got_ref[...].astype(F32)
    group = [got[:, 8 * g : 8 * g + 8, :] for g in range(4)]
    row = iota((parts, 8, LANES), 1)
    halo = jnp.where(
        row < 2,
        pltpu.roll(group[0], 2, 1),
        jnp.where(row < 4, pltpu.roll(group[1], 4, 1), pltpu.roll(group[2], 6, 1)),
    )
    columns = [x.reshape(slots, LANES) for x in group + [halo]]

    at = iota((2 * parts, slots), 1) - 8 * (iota((2 * parts, slots), 0) % parts)
    take = (at == 6 + iota((2 * parts, slots), 0) // parts).astype(F32).astype(BF16)
    ends = dot(take, columns[3].astype(BF16))
    ends = (8.0 * ends + pltpu.roll(ends, 64, 1)).astype(jnp.int32)
    lane = iota((parts, slots), 1)
    for k in range(pair_count):
        first = (ends[0:parts, k : k + 1] == lane).astype(F32)
        second = (ends[parts : 2 * parts, k : k + 1] == lane).astype(F32)
        at = pl.ds(k * parts, parts)
        for ref, value in ((first_ref, first), (second_ref, second), (diff_ref, second - first)):
            value = value.astype(BF16)
            ref[at, :] = jnp.concatenate([value, value], axis=1)
    diff_t = jnp.transpose(diff_ref[:, 0:slots].astype(F32)).astype(BF16)
    diff_t_ref[...] = jnp.concatenate([diff_t, diff_t], axis=1)

    def main_place(shape, dim):
        p = iota(shape, dim)
        lane = p % LANES
        k = (lane // width - me + 64) % blocks
        line = jnp.where(k < 4, (p // LANES) * 4 + k, 1000 * (dim + 1))
        return line, lane % width

    def halo_place(shape, dim):
        p = iota(shape, dim)
        t = (p // 8 - me + 64) % 16
        j = p % 8
        return t % 8, jnp.where(j < HALO, j - HALO, width + j - HALO), t // 8

    to_line, to_col = main_place((1, 2 * LANES), 1)

    def near(line, col):
        hit = (jnp.abs(line - to_line) <= 1) & (jnp.abs(col - to_col) <= HALO)
        return hit.astype(F32)

    band = near(*main_place((2 * LANES, 1), 0)).astype(BF16)
    line, col, imag = halo_place((LANES, 1), 0)
    band_halo = near(line, col)
    band_cross = (band_halo * (2.0 * imag.astype(F32) - 1.0)).astype(BF16)
    band_halo = band_halo.astype(BF16)
    band_halo = jnp.concatenate([band, band, band_halo, band_halo], axis=0)
    band_cross = jnp.concatenate([band, band, band_cross, band_cross], axis=0)

    def looks(field, edge, table):
        return dot(jnp.concatenate([*split(field), *split(edge)], axis=1), table)

    re = jnp.concatenate(columns[0:2], axis=1)
    im = jnp.concatenate(columns[2:4], axis=1)
    power_high, power_low = split(looks(re * re + im * im, columns[4] * columns[4], band_halo))
    tiles = jnp.concatenate([x.astype(BF16) for x in columns], axis=1)
    swap = pltpu.roll(columns[4], 64, 1).astype(BF16)
    zero = jnp.zeros_like(tiles)
    first_tiles = jnp.concatenate(
        [
            jnp.concatenate([power_high, tiles], axis=1),
            jnp.concatenate([power_low, zero], axis=1),
        ],
        axis=0,
    )
    second_tiles = jnp.concatenate(
        [
            jnp.concatenate([power_high, tiles, swap], axis=1),
            jnp.concatenate([power_low, zero, jnp.zeros_like(swap)], axis=1),
        ],
        axis=0,
    )

    def body(step, carry):
        at = pl.ds(pl.multiple_of(step * chunk, 16), chunk)
        u = dot(first_ref[at, :], first_tiles)
        v = dot(second_ref[at, :], second_tiles)
        u_power, u_re, u_im, u_halo = u[:, 0:256], u[:, 256:512], u[:, 512:768], u[:, 768:896]
        v_power, v_re, v_im, v_halo = v[:, 0:256], v[:, 256:512], v[:, 512:768], v[:, 768:896]
        real = looks(u_re * v_re + u_im * v_im, u_halo * v_halo, band_halo)
        imag = looks(u_im * v_re - u_re * v_im, u_halo * v[:, 896:1024], band_cross)
        scale = lax.rsqrt(jnp.maximum(u_power * v_power, 1.0))
        real = real * scale
        imag = imag * scale
        weight = real * real + imag * imag
        weight_ref[at, :] = weight
        high, low = split(weight * imag)
        term_ref[at, :] = high
        term_ref[pl.ds(pl.multiple_of(pairs + step * chunk, 16), chunk), :] = low
        return carry

    if chunk == pairs:
        body(0, 0)
    else:
        lax.fori_loop(0, pairs // chunk, body, 0)

    right_side = dot(diff_t_ref[...], term_ref[...])

    def operator(field):
        high, low = split(field)
        spread = dot(diff_ref[...], jnp.concatenate([high, low], axis=0))
        high, low = split(weight_ref[...] * spread)
        term_ref[0:pairs, :] = high
        term_ref[pairs : 2 * pairs, :] = low
        return DAMPING * field + dot(diff_t_ref[...], term_ref[...])

    def inner(a, b):
        return jnp.sum(a * b, axis=0, keepdims=True)

    solution = jnp.zeros_like(right_side)
    residual = right_side
    direction = right_side
    norm_now = inner(residual, residual)
    for step in range(ITERS):
        image = operator(direction)
        step_size = norm_now / (inner(direction, image) + EPSILON)
        solution = solution + step_size * direction
        residual = residual - step_size * image
        if step + 1 < ITERS:
            norm_next = inner(residual, residual)
            direction = residual + norm_next / (norm_now + EPSILON) * direction
            norm_now = norm_next
    row = iota((parts, 8, LANES), 1)
    groups = []
    for field in (solution, residual):
        field = field.reshape(parts, 8, 2 * LANES)
        for h in range(2):
            part = field[:, :, h * LANES : (h + 1) * LANES]
            largest = jnp.max(jnp.abs(part), axis=1, keepdims=True)
            power = jnp.floor(jnp.log2(jnp.maximum(largest, 2.0**-126))) + 1.0
            coded = jnp.floor(part * jnp.exp2(-power) * 32768.0 + 0.5)
            coded = jnp.where(row == 6, power, jnp.clip(coded, -32767.0, 32767.0))
            groups.append(coded.astype(jnp.int32))
    out_ref[...] = jnp.concatenate(groups, axis=1).astype(jnp.int16)


def unpack_kernel(got_ref, *out_refs):
    parts = got_ref.shape[0]
    dates, rows, cols = out_refs[0].shape
    width = cols // parts
    blocks = LANES // width
    block = iota((8, LANES), 1) // width
    got = got_ref[...].astype(jnp.int32).astype(F32)
    for o, out_ref in enumerate(out_refs):
        for h in range(2):
            at = (2 * o + h) * 8
            part = got[:, at : at + 8, :] * 2.0**-15 * jnp.exp2(got[:, at + 6 : at + 7, :])
            for tile in range(cols // LANES):
                for k in range(4):
                    total = jnp.zeros((8, LANES), F32)
                    for q in range(blocks):
                        total = jnp.where(block == (q + k) % blocks, part[tile * blocks + q], total)
                    shift = -width * k % LANES
                    if shift:
                        total = pltpu.roll(total, shift, 1)
                    out_ref[:, 4 * h + k, tile * LANES : (tile + 1) * LANES] = total[0:dates]


def shards(slc, line_mask, pair_dev, pair_slot):
    parts = lax.axis_size("date")
    dates, _, rows, cols = slc.shape
    pair_count = pair_dev.shape[0]
    pairs = parts * pair_count
    width = cols // parts
    chunk = max(c for c in range(16, 513, 16) if pairs % c == 0)
    vmem = pl.BlockSpec(memory_space=pltpu.VMEM)

    packed = pl.pallas_call(
        pack_kernel,
        out_shape=jax.ShapeDtypeStruct((parts, 32, LANES), BF16),
        in_specs=[pl.BlockSpec(memory_space=pltpu.HBM)] * 4,
        out_specs=vmem,
        scratch_shapes=[
            pltpu.VMEM((dates, rows), jnp.int32),
            pltpu.VMEM((2, pair_count), jnp.int32),
            pltpu.VMEM((2, pair_count), jnp.int32),
            pltpu.VMEM(slc.shape, BF16),
            pltpu.VMEM((cols, 8 * parts), BF16),
            pltpu.SemaphoreType.DMA((6,)),
        ],
        compiler_params=pltpu.CompilerParams(vmem_limit_bytes=4 * 1024 * 1024),
        name="pack",
    )(
        *[
            pltpu.with_memory_space_constraint(x, pltpu.HBM)
            for x in (line_mask, pair_dev.T, pair_slot.T, slc)
        ]
    )
    got = lax.all_to_all(packed, "date", split_axis=0, concat_axis=0, tiled=True)
    fields = pl.pallas_call(
        functools.partial(strip_kernel, dates, pair_count, width, chunk),
        out_shape=jax.ShapeDtypeStruct((parts, 32, LANES), jnp.int16),
        in_specs=[vmem],
        out_specs=vmem,
        scratch_shapes=[
            pltpu.VMEM((pairs, 16 * parts), BF16),
            pltpu.VMEM((pairs, 16 * parts), BF16),
            pltpu.VMEM((pairs, 16 * parts), BF16),
            pltpu.VMEM((8 * parts, 2 * pairs), BF16),
            pltpu.VMEM((pairs, 2 * LANES), F32),
            pltpu.VMEM((2 * pairs, 2 * LANES), BF16),
        ],
        compiler_params=pltpu.CompilerParams(vmem_limit_bytes=24 * 1024 * 1024),
        name="strip",
    )(got)
    back = lax.all_to_all(fields, "date", split_axis=0, concat_axis=0, tiled=True)
    out = jax.ShapeDtypeStruct((dates, rows, cols), F32)
    return pl.pallas_call(
        unpack_kernel,
        out_shape=(out, out),
        in_specs=[vmem],
        out_specs=(vmem, vmem),
        compiler_params=pltpu.CompilerParams(vmem_limit_bytes=4 * 1024 * 1024),
        name="unpack",
    )(back)


def solution(mesh):
    in_specs = (P("date", None, "grp", None), P("date", "grp"), P("date", None), P("date", None))
    out_specs = (P("date", "grp", None), P("date", "grp", None))
    return jax.shard_map(shards, mesh=mesh, in_specs=in_specs, out_specs=out_specs, check_vma=False)
```

```python
import functools

import jax
import jax.numpy as jnp
from jax import lax
from jax.experimental import pallas as pl
from jax.experimental.pallas import tpu as pltpu
from jax.sharding import PartitionSpec as P

ITERS = 2
DAMPING = 0.5
EPSILON = 1e-06
LANES = 128
HALO = 4
F32 = jnp.float32
BF16 = jnp.bfloat16


def iota(shape, dim):
    return lax.broadcasted_iota(jnp.int32, shape, dim)


def dot(a, b):
    return lax.dot_general(a, b, (((1,), (0,)), ((), ())), preferred_element_type=F32)


def split(x):
    high = x.astype(BF16)
    return high, (x - high.astype(F32)).astype(BF16)


def make_table(width, table_ref):
    blocks = LANES // width
    me = lax.axis_index("date")

    def main_place(shape, dim):
        p = iota(shape, dim)
        lane = p % LANES
        k = (lane // width - me + 64) % blocks
        line = jnp.where(k < 4, (p // LANES) * 4 + k, 1000 * (dim + 1))
        return line, lane % width

    def halo_place(shape, dim):
        p = iota(shape, dim)
        t = (p // 8 - me + 64) % 16
        j = p % 8
        return t % 8, jnp.where(j < HALO, j - HALO, width + j - HALO), t // 8

    to_line, to_col = main_place((1, 2 * LANES), 1)

    def near(line, col):
        hit = (jnp.abs(line - to_line) <= 1) & (jnp.abs(col - to_col) <= HALO)
        return hit.astype(F32)

    table_ref[0:256, :] = near(*main_place((2 * LANES, 1), 0)).astype(BF16)
    line, col, imag = halo_place((LANES, 1), 0)
    halo = near(line, col)
    table_ref[256:384, :] = halo.astype(BF16)
    table_ref[384:512, :] = (halo * (2.0 * imag.astype(F32) - 1.0)).astype(BF16)


def pack_kernel(mask_in, dev_in, slot_in, slc_in, out_ref, table_ref, mask_ref, dev_ref, slot_ref, slc_ref, side_ref, sems):
    step = slc_ref.shape[0] // 3
    copies = [
        pltpu.make_async_copy(source, target, sems.at[n])
        for n, (source, target) in enumerate(
            [(mask_in, mask_ref), (dev_in, dev_ref), (slot_in, slot_ref)]
            + [
                (slc_in.at[pl.ds(a, step)], slc_ref.at[pl.ds(a, step)])
                for a in range(0, slc_ref.shape[0], step)
            ]
        )
    ]
    for copy in copies:
        copy.start()
    parts = out_ref.shape[0]
    dates, _, rows, cols = slc_ref.shape
    width = cols // parts
    blocks = LANES // width
    make_table(width, table_ref)
    place = iota((cols, 8 * parts), 1)
    j = place % 8
    column = (place // 8) * width + jnp.where(j < HALO, j - HALO, width + j - HALO)
    side_ref[...] = (iota((cols, 8 * parts), 0) == column).astype(F32).astype(BF16)
    for copy in copies[:3]:
        copy.wait()
    mask = jnp.concatenate(
        [mask_ref[...].astype(F32), jnp.zeros((8 - dates, rows), F32)], axis=0
    )
    lane = iota((8, dates * 2 * rows), 1)
    row = iota((8, dates * 2 * rows), 0)
    picks = []
    for i in range(rows):
        for c in range(2):
            picks.append(jnp.where(lane == (row * 2 + c) * rows + i, mask[:, i : i + 1], 0.0))
    pick = jnp.concatenate(picks, axis=0).astype(BF16)
    for copy in copies[3:]:
        copy.wait()
    tiles = slc_ref[...].astype(F32).reshape(dates * 2 * rows, cols).astype(BF16)
    lines = dot(pick, tiles)
    edges = dot(lines.astype(BF16), side_ref[...])

    lane = iota((8, LANES), 1)
    row = iota((8, LANES), 0)
    block = lane // width
    block8 = lane // 8
    pair_count = dev_ref.shape[1]
    spare = jnp.zeros((2, 64 - pair_count), F32)
    index_rows = jnp.concatenate(
        [dev_ref[...].astype(F32), spare, slot_ref[...].astype(F32), spare], axis=1
    )
    index_rows = jnp.concatenate([jnp.zeros((6, LANES), F32), index_rows], axis=0)

    def rolled(array, i, c, tile, shift):
        at = (i * 2 + c) * 8
        part = array[at : at + 8, tile * LANES : (tile + 1) * LANES]
        return part if shift % LANES == 0 else pltpu.roll(part, shift % LANES, 1)

    for tile in range(cols // LANES):
        main = {
            (c, h, k): rolled(lines, 4 * h + k, c, tile, width * k)
            for c in range(2)
            for h in range(2)
            for k in range(4)
        }
        for q in range(blocks):
            e = tile * blocks + q
            groups = []
            for c in range(2):
                for h in range(2):
                    total = jnp.zeros((8, LANES), F32)
                    for k in range(4):
                        total = jnp.where(block == (q + k) % blocks, main[c, h, k], total)
                    groups.append(total)
            halo = jnp.zeros((8, LANES), F32)
            for i in range(rows):
                for c in range(2):
                    moved = rolled(edges, i, c, e // 16, 8 * (i + 8 * c))
                    halo = jnp.where(block8 == (e + i + 8 * c) % 16, moved, halo)
            for g in range(3):
                groups[g] = jnp.where(row >= 6, pltpu.roll(halo, 6 - 2 * g, 0), groups[g])
            groups[3] = jnp.where(row >= 6, index_rows, groups[3])
            out_ref[e] = jnp.concatenate(groups, axis=0).astype(BF16)


def strip_kernel(
    pair_count, chunk, got_ref, table_ref, out_ref, first_ref, second_ref, diff_ref, diff_t_ref, weight_ref, term_ref
):
    parts = got_ref.shape[0]
    slots = 8 * parts
    pairs = parts * pair_count

    got = got_ref[...].astype(F32)
    group = [got[:, 8 * g : 8 * g + 8, :] for g in range(4)]
    row = iota((parts, 8, LANES), 1)
    halo = jnp.where(
        row < 2,
        pltpu.roll(group[0], 2, 1),
        jnp.where(row < 4, pltpu.roll(group[1], 4, 1), pltpu.roll(group[2], 6, 1)),
    )
    columns = [x.reshape(slots, LANES) for x in group + [halo]]

    at = iota((2 * parts, slots), 1) - 8 * (iota((2 * parts, slots), 0) % parts)
    take = (at == 6 + iota((2 * parts, slots), 0) // parts).astype(F32).astype(BF16)
    ends = dot(take, columns[3].astype(BF16))
    ends = (8.0 * ends + pltpu.roll(ends, 64, 1)).astype(jnp.int32)
    lane = iota((parts, slots), 1)
    for k in range(pair_count):
        first = (ends[0:parts, k : k + 1] == lane).astype(F32)
        second = (ends[parts : 2 * parts, k : k + 1] == lane).astype(F32)
        at = pl.ds(k * parts, parts)
        for ref, value in ((first_ref, first), (second_ref, second), (diff_ref, second - first)):
            value = value.astype(BF16)
            ref[at, :] = jnp.concatenate([value, value], axis=1)
    diff_t = jnp.transpose(diff_ref[:, 0:slots].astype(F32)).astype(BF16)
    diff_t_ref[...] = jnp.concatenate([diff_t, diff_t], axis=1)

    band, halo, cross = table_ref[0:256, :], table_ref[256:384, :], table_ref[384:512, :]
    band_halo = jnp.concatenate([band, band, halo, halo], axis=0)
    band_cross = jnp.concatenate([band, band, cross, cross], axis=0)

    def looks(field, edge, table):
        return dot(jnp.concatenate([*split(field), *split(edge)], axis=1), table)

    re = jnp.concatenate(columns[0:2], axis=1)
    im = jnp.concatenate(columns[2:4], axis=1)
    power_high, power_low = split(looks(re * re + im * im, columns[4] * columns[4], band_halo))
    tiles = jnp.concatenate([x.astype(BF16) for x in columns], axis=1)
    swap = pltpu.roll(columns[4], 64, 1).astype(BF16)
    zero = jnp.zeros_like(tiles)
    first_tiles = jnp.concatenate(
        [
            jnp.concatenate([power_high, tiles], axis=1),
            jnp.concatenate([power_low, zero], axis=1),
        ],
        axis=0,
    )
    second_tiles = jnp.concatenate(
        [
            jnp.concatenate([power_high, tiles, swap], axis=1),
            jnp.concatenate([power_low, zero, jnp.zeros_like(swap)], axis=1),
        ],
        axis=0,
    )

    def body(step, carry):
        at = pl.ds(pl.multiple_of(step * chunk, 16), chunk)
        u = dot(first_ref[at, :], first_tiles)
        v = dot(second_ref[at, :], second_tiles)
        u_power, u_re, u_im, u_halo = u[:, 0:256], u[:, 256:512], u[:, 512:768], u[:, 768:896]
        v_power, v_re, v_im, v_halo = v[:, 0:256], v[:, 256:512], v[:, 512:768], v[:, 768:896]
        real = looks(u_re * v_re + u_im * v_im, u_halo * v_halo, band_halo)
        imag = looks(u_im * v_re - u_re * v_im, u_halo * v[:, 896:1024], band_cross)
        scale = lax.rsqrt(jnp.maximum(u_power * v_power, 1.0))
        real = real * scale
        imag = imag * scale
        weight = real * real + imag * imag
        weight_ref[at, :] = weight
        high, low = split(weight * imag)
        term_ref[at, :] = high
        term_ref[pl.ds(pl.multiple_of(pairs + step * chunk, 16), chunk), :] = low
        return carry

    if chunk == pairs:
        body(0, 0)
    else:
        lax.fori_loop(0, pairs // chunk, body, 0)

    right_side = dot(diff_t_ref[...], term_ref[...])

    def operator(field):
        high, low = split(field)
        spread = dot(diff_ref[...], jnp.concatenate([high, low], axis=0))
        high, low = split(weight_ref[...] * spread)
        term_ref[0:pairs, :] = high
        term_ref[pairs : 2 * pairs, :] = low
        return DAMPING * field + dot(diff_t_ref[...], term_ref[...])

    def inner(a, b):
        return jnp.sum(a * b, axis=0, keepdims=True)

    solution = jnp.zeros_like(right_side)
    residual = right_side
    direction = right_side
    norm_now = inner(residual, residual)
    for step in range(ITERS):
        image = operator(direction)
        step_size = norm_now / (inner(direction, image) + EPSILON)
        solution = solution + step_size * direction
        residual = residual - step_size * image
        if step + 1 < ITERS:
            norm_next = inner(residual, residual)
            direction = residual + norm_next / (norm_now + EPSILON) * direction
            norm_now = norm_next
    row = iota((parts, 8, LANES), 1)
    groups = []
    for field in (solution, residual):
        field = field.reshape(parts, 8, 2 * LANES)
        for h in range(2):
            part = field[:, :, h * LANES : (h + 1) * LANES]
            largest = jnp.max(jnp.abs(part), axis=1, keepdims=True)
            power = jnp.floor(jnp.log2(jnp.maximum(largest, 2.0**-126))) + 1.0
            coded = jnp.floor(part * jnp.exp2(-power) * 32768.0 + 0.5)
            coded = jnp.where(row == 6, power, jnp.clip(coded, -32767.0, 32767.0))
            groups.append(coded.astype(jnp.int32))
    out_ref[...] = jnp.concatenate(groups, axis=1).astype(jnp.int16)


def unpack_kernel(got_ref, *out_refs):
    parts = got_ref.shape[0]
    dates, rows, cols = out_refs[0].shape
    width = cols // parts
    blocks = LANES // width
    block = iota((8, LANES), 1) // width
    got = got_ref[...].astype(jnp.int32).astype(F32)
    for o, out_ref in enumerate(out_refs):
        for h in range(2):
            at = (2 * o + h) * 8
            part = got[:, at : at + 8, :] * 2.0**-15 * jnp.exp2(got[:, at + 6 : at + 7, :])
            for tile in range(cols // LANES):
                for k in range(4):
                    total = jnp.zeros((8, LANES), F32)
                    for q in range(blocks):
                        total = jnp.where(block == (q + k) % blocks, part[tile * blocks + q], total)
                    shift = -width * k % LANES
                    if shift:
                        total = pltpu.roll(total, shift, 1)
                    out_ref[:, 4 * h + k, tile * LANES : (tile + 1) * LANES] = total[0:dates]


def shards(slc, line_mask, pair_dev, pair_slot):
    parts = lax.axis_size("date")
    dates, _, rows, cols = slc.shape
    pair_count = pair_dev.shape[0]
    pairs = parts * pair_count
    width = cols // parts
    chunk = max(c for c in range(16, 513, 16) if pairs % c == 0)
    vmem = pl.BlockSpec(memory_space=pltpu.VMEM)

    packed, table = pl.pallas_call(
        pack_kernel,
        out_shape=(
            jax.ShapeDtypeStruct((parts, 32, LANES), BF16),
            jax.ShapeDtypeStruct((4 * LANES, 2 * LANES), BF16),
        ),
        in_specs=[pl.BlockSpec(memory_space=pltpu.HBM)] * 4,
        out_specs=(vmem, vmem),
        scratch_shapes=[
            pltpu.VMEM((dates, rows), jnp.int32),
            pltpu.VMEM((2, pair_count), jnp.int32),
            pltpu.VMEM((2, pair_count), jnp.int32),
            pltpu.VMEM(slc.shape, BF16),
            pltpu.VMEM((cols, 8 * parts), BF16),
            pltpu.SemaphoreType.DMA((6,)),
        ],
        compiler_params=pltpu.CompilerParams(vmem_limit_bytes=4 * 1024 * 1024),
        name="pack",
    )(
        *[
            pltpu.with_memory_space_constraint(x, pltpu.HBM)
            for x in (line_mask, pair_dev.T, pair_slot.T, slc)
        ]
    )
    got = lax.all_to_all(packed, "date", split_axis=0, concat_axis=0, tiled=True)
    fields = pl.pallas_call(
        functools.partial(strip_kernel, pair_count, chunk),
        out_shape=jax.ShapeDtypeStruct((parts, 32, LANES), jnp.int16),
        in_specs=[vmem] * 2,
        out_specs=vmem,
        scratch_shapes=[
            pltpu.VMEM((pairs, 16 * parts), BF16),
            pltpu.VMEM((pairs, 16 * parts), BF16),
            pltpu.VMEM((pairs, 16 * parts), BF16),
            pltpu.VMEM((8 * parts, 2 * pairs), BF16),
            pltpu.VMEM((pairs, 2 * LANES), F32),
            pltpu.VMEM((2 * pairs, 2 * LANES), BF16),
        ],
        compiler_params=pltpu.CompilerParams(vmem_limit_bytes=24 * 1024 * 1024),
        name="strip",
    )(got, table)
    back = lax.all_to_all(fields, "date", split_axis=0, concat_axis=0, tiled=True)
    out = jax.ShapeDtypeStruct((dates, rows, cols), F32)
    return pl.pallas_call(
        unpack_kernel,
        out_shape=(out, out),
        in_specs=[vmem],
        out_specs=(vmem, vmem),
        compiler_params=pltpu.CompilerParams(vmem_limit_bytes=4 * 1024 * 1024),
        name="unpack",
    )(back)


def solution(mesh):
    in_specs = (P("date", None, "grp", None), P("date", "grp"), P("date", None), P("date", None))
    out_specs = (P("date", "grp", None), P("date", "grp", None))
    return jax.shard_map(shards, mesh=mesh, in_specs=in_specs, out_specs=out_specs, check_vma=False)
```

```python
import functools

import jax
import jax.numpy as jnp
from jax import lax
from jax.experimental import pallas as pl
from jax.experimental.pallas import tpu as pltpu
from jax.sharding import PartitionSpec as P

ITERS = 2
DAMPING = 0.5
EPSILON = 1e-06
LANES = 128
HALO = 4
F32 = jnp.float32
BF16 = jnp.bfloat16


def iota(shape, dim):
    return lax.broadcasted_iota(jnp.int32, shape, dim)


def dot(a, b):
    return lax.dot_general(a, b, (((1,), (0,)), ((), ())), preferred_element_type=F32)


def split(x):
    high = x.astype(BF16)
    return high, (x - high.astype(F32)).astype(BF16)


def make_table(width, table_ref):
    blocks = LANES // width
    me = lax.axis_index("date")

    def main_place(shape, dim):
        p = iota(shape, dim)
        lane = p % LANES
        k = (lane // width - me + 64) % blocks
        line = jnp.where(k < 4, (p // LANES) * 4 + k, 1000 * (dim + 1))
        return line, lane % width

    def halo_place(shape, dim):
        p = iota(shape, dim)
        t = (p // 8 - me + 64) % 16
        j = p % 8
        return t % 8, jnp.where(j < HALO, j - HALO, width + j - HALO), t // 8

    to_line, to_col = main_place((1, 2 * LANES), 1)

    def near(line, col):
        hit = (jnp.abs(line - to_line) <= 1) & (jnp.abs(col - to_col) <= HALO)
        return hit.astype(F32)

    table_ref[0:256, :] = near(*main_place((2 * LANES, 1), 0)).astype(BF16)
    line, col, imag = halo_place((LANES, 1), 0)
    halo = near(line, col)
    table_ref[256:384, :] = halo.astype(BF16)
    table_ref[384:512, :] = (halo * (2.0 * imag.astype(F32) - 1.0)).astype(BF16)


def pack_kernel(mask_in, dev_in, slot_in, slc_in, out_ref, table_ref, mask_ref, dev_ref, slot_ref, slc_ref, side_ref, sems):
    step = slc_ref.shape[0] // 3
    copies = [
        pltpu.make_async_copy(source, target, sems.at[n])
        for n, (source, target) in enumerate(
            [(mask_in, mask_ref), (dev_in, dev_ref), (slot_in, slot_ref)]
            + [
                (slc_in.at[pl.ds(a, step)], slc_ref.at[pl.ds(a, step)])
                for a in range(0, slc_ref.shape[0], step)
            ]
        )
    ]
    for copy in copies:
        copy.start()
    parts = out_ref.shape[0]
    dates, _, rows, cols = slc_ref.shape
    width = cols // parts
    blocks = LANES // width
    make_table(width, table_ref)
    place = iota((cols, 8 * parts), 1)
    j = place % 8
    column = (place // 8) * width + jnp.where(j < HALO, j - HALO, width + j - HALO)
    side_ref[...] = (iota((cols, 8 * parts), 0) == column).astype(F32).astype(BF16)
    for copy in copies[:3]:
        copy.wait()
    mask = jnp.concatenate(
        [mask_ref[...].astype(F32), jnp.zeros((8 - dates, rows), F32)], axis=0
    )
    lane = iota((8, dates * 2 * rows), 1)
    row = iota((8, dates * 2 * rows), 0)
    picks = []
    for i in range(rows):
        for c in range(2):
            picks.append(jnp.where(lane == (row * 2 + c) * rows + i, mask[:, i : i + 1], 0.0))
    pick = jnp.concatenate(picks, axis=0).astype(BF16)
    for copy in copies[3:]:
        copy.wait()
    tiles = slc_ref[...].astype(F32).reshape(dates * 2 * rows, cols).astype(BF16)
    lines = dot(pick, tiles)
    edges = dot(lines.astype(BF16), side_ref[...])

    lane = iota((8, LANES), 1)
    row = iota((8, LANES), 0)
    block = lane // width
    block8 = lane // 8
    pair_count = dev_ref.shape[1]
    spare = jnp.zeros((2, 64 - pair_count), F32)
    index_rows = jnp.concatenate(
        [dev_ref[...].astype(F32), spare, slot_ref[...].astype(F32), spare], axis=1
    )
    index_rows = jnp.concatenate([jnp.zeros((6, LANES), F32), index_rows], axis=0)

    def rolled(array, i, c, tile, shift):
        at = (i * 2 + c) * 8
        part = array[at : at + 8, tile * LANES : (tile + 1) * LANES]
        return part if shift % LANES == 0 else pltpu.roll(part, shift % LANES, 1)

    for tile in range(cols // LANES):
        main = {
            (c, h, k): rolled(lines, 4 * h + k, c, tile, width * k)
            for c in range(2)
            for h in range(2)
            for k in range(4)
        }
        for q in range(blocks):
            e = tile * blocks + q
            groups = []
            for c in range(2):
                for h in range(2):
                    total = jnp.zeros((8, LANES), F32)
                    for k in range(4):
                        total = jnp.where(block == (q + k) % blocks, main[c, h, k], total)
                    groups.append(total)
            halo = jnp.zeros((8, LANES), F32)
            for i in range(rows):
                for c in range(2):
                    moved = rolled(edges, i, c, e // 16, 8 * (i + 8 * c))
                    halo = jnp.where(block8 == (e + i + 8 * c) % 16, moved, halo)
            for g in range(3):
                groups[g] = jnp.where(row >= 6, pltpu.roll(halo, 6 - 2 * g, 0), groups[g])
            groups[3] = jnp.where(row >= 6, index_rows, groups[3])
            out_ref[e] = jnp.concatenate(groups, axis=0).astype(BF16)


def strip_kernel(
    pair_count, chunk, got_ref, table_ref, out_ref, first_ref, second_ref, diff_ref, diff_t_ref, weight_ref, term_ref
):
    parts = got_ref.shape[0]
    slots = 8 * parts
    pairs = parts * pair_count

    got = got_ref[...].astype(F32)
    group = [got[:, 8 * g : 8 * g + 8, :] for g in range(4)]
    row = iota((parts, 8, LANES), 1)
    halo = jnp.where(
        row < 2,
        pltpu.roll(group[0], 2, 1),
        jnp.where(row < 4, pltpu.roll(group[1], 4, 1), pltpu.roll(group[2], 6, 1)),
    )
    columns = [x.reshape(slots, LANES) for x in group + [halo]]

    at = iota((2 * parts, slots), 1) - 8 * (iota((2 * parts, slots), 0) % parts)
    take = (at == 6 + iota((2 * parts, slots), 0) // parts).astype(F32).astype(BF16)
    ends = dot(take, columns[3].astype(BF16))
    ends = (8.0 * ends + pltpu.roll(ends, 64, 1)).astype(jnp.int32)
    lane = iota((parts, slots), 1)
    for k in range(pair_count):
        first = (ends[0:parts, k : k + 1] == lane).astype(F32)
        second = (ends[parts : 2 * parts, k : k + 1] == lane).astype(F32)
        at = pl.ds(k * parts, parts)
        for ref, value in ((first_ref, first), (second_ref, second), (diff_ref, second - first)):
            value = value.astype(BF16)
            ref[at, :] = jnp.concatenate([value, value], axis=1)
    diff_t_ref[...] = jnp.transpose(diff_ref[:, 0:slots].astype(F32)).astype(BF16)

    band, halo, cross = table_ref[0:256, :], table_ref[256:384, :], table_ref[384:512, :]
    band_halo = jnp.concatenate([band, band, halo, halo], axis=0)
    band_cross = jnp.concatenate([band, band, cross, cross], axis=0)

    def looks(field, edge, table):
        return dot(jnp.concatenate([*split(field), *split(edge)], axis=1), table)

    re = jnp.concatenate(columns[0:2], axis=1)
    im = jnp.concatenate(columns[2:4], axis=1)
    power_high, power_low = split(looks(re * re + im * im, columns[4] * columns[4], band_halo))
    tiles = jnp.concatenate([x.astype(BF16) for x in columns], axis=1)
    zero = jnp.zeros_like(tiles)
    both_tiles = jnp.concatenate(
        [
            jnp.concatenate([power_high, tiles[:, 0:512]], axis=1),
            jnp.concatenate([power_low, zero[:, 0:512]], axis=1),
        ],
        axis=0,
    )
    none = jnp.zeros((slots, LANES), BF16)
    halo_tiles = jnp.concatenate(
        [
            jnp.concatenate([tiles[:, 512:640], none], axis=1),
            jnp.concatenate([none, tiles[:, 512:640]], axis=1),
        ],
        axis=0,
    )

    def body(step, carry):
        at = pl.ds(pl.multiple_of(step * chunk, 16), chunk)
        u = dot(first_ref[at, :], both_tiles)
        v = dot(second_ref[at, :], both_tiles)
        u_power, u_re, u_im = u[:, 0:256], u[:, 256:512], u[:, 512:768]
        v_power, v_re, v_im = v[:, 0:256], v[:, 256:512], v[:, 512:768]
        either = jnp.concatenate([first_ref[at, 0:slots], second_ref[at, 0:slots]], axis=1)
        halos = dot(either, halo_tiles)
        u_halo, v_halo = halos[:, 0:128], halos[:, 128:256]
        real = looks(u_re * v_re + u_im * v_im, u_halo * v_halo, band_halo)
        imag = looks(u_im * v_re - u_re * v_im, u_halo * pltpu.roll(v_halo, 64, 1), band_cross)
        scale = lax.rsqrt(jnp.maximum(u_power * v_power, 1.0))
        real = real * scale
        imag = imag * scale
        weight = real * real + imag * imag
        weight_ref[at, :] = weight
        high, low = split(weight * imag)
        term_ref[at, :] = high
        term_ref[pl.ds(pl.multiple_of(pairs + step * chunk, 16), chunk), :] = low
        return carry

    if chunk == pairs:
        body(0, 0)
    else:
        lax.fori_loop(0, pairs // chunk, body, 0)

    right_side = dot(diff_t_ref[...], term_ref[0:pairs, :])
    right_side = right_side + dot(diff_t_ref[...], term_ref[pairs : 2 * pairs, :])

    def inner(a, b):
        return jnp.sum(a * b, axis=0, keepdims=True)

    half = -(-pairs // 32) * 16
    halves = (slice(0, half), slice(half, pairs))

    def operator(field):
        high, low = split(field)
        both = jnp.concatenate([high, low], axis=0)
        image = DAMPING * field
        curve = DAMPING * inner(field, field)
        for at in halves:
            spread = dot(diff_ref[at, :], both)
            term = weight_ref[at, :] * spread
            curve = curve + inner(term, spread)
            high, low = split(term)
            image = image + dot(diff_t_ref[:, at], high) + dot(diff_t_ref[:, at], low)
        return image, curve

    solution = jnp.zeros_like(right_side)
    residual = right_side
    direction = right_side
    norm_now = inner(residual, residual)
    for step in range(ITERS):
        image, curve = operator(direction)
        step_size = norm_now / (curve + EPSILON)
        solution = solution + step_size * direction
        residual = residual - step_size * image
        if step + 1 < ITERS:
            norm_next = inner(residual, residual)
            direction = residual + norm_next / (norm_now + EPSILON) * direction
            norm_now = norm_next
    row = iota((parts, 8, LANES), 1)
    groups = []
    for field in (solution, residual):
        field = field.reshape(parts, 8, 2 * LANES)
        for h in range(2):
            part = field[:, :, h * LANES : (h + 1) * LANES]
            largest = jnp.max(jnp.abs(part), axis=1, keepdims=True)
            power = jnp.floor(jnp.log2(jnp.maximum(largest, 2.0**-126))) + 1.0
            coded = jnp.floor(part * jnp.exp2(-power) * 32768.0 + 0.5)
            coded = jnp.where(row == 6, power, jnp.clip(coded, -32767.0, 32767.0))
            groups.append(coded.astype(jnp.int32))
    out_ref[...] = jnp.concatenate(groups, axis=1).astype(jnp.int16)


def unpack_kernel(got_ref, *out_refs):
    parts = got_ref.shape[0]
    dates, rows, cols = out_refs[0].shape
    width = cols // parts
    blocks = LANES // width
    block = iota((8, LANES), 1) // width
    got = got_ref[...].astype(jnp.int32).astype(F32)
    for o, out_ref in enumerate(out_refs):
        lines = [[] for _ in range(cols // LANES)]
        for h in range(2):
            at = (2 * o + h) * 8
            part = got[:, at : at + 8, :] * 2.0**-15 * jnp.exp2(got[:, at + 6 : at + 7, :])
            for tile in range(cols // LANES):
                for k in range(4):
                    total = jnp.zeros((8, LANES), F32)
                    for q in range(blocks):
                        total = jnp.where(block == (q + k) % blocks, part[tile * blocks + q], total)
                    shift = -width * k % LANES
                    if shift:
                        total = pltpu.roll(total, shift, 1)
                    lines[tile].append(total)
        for tile in range(cols // LANES):
            whole = jnp.swapaxes(jnp.stack(lines[tile], axis=0), 0, 1)
            out_ref[:, :, tile * LANES : (tile + 1) * LANES] = whole[0:dates]


def shards(slc, line_mask, pair_dev, pair_slot):
    parts = lax.axis_size("date")
    dates, _, rows, cols = slc.shape
    pair_count = pair_dev.shape[0]
    pairs = parts * pair_count
    width = cols // parts
    chunk = max(c for c in range(16, 513, 16) if pairs % c == 0)
    vmem = pl.BlockSpec(memory_space=pltpu.VMEM)

    packed, table = pl.pallas_call(
        pack_kernel,
        out_shape=(
            jax.ShapeDtypeStruct((parts, 32, LANES), BF16),
            jax.ShapeDtypeStruct((4 * LANES, 2 * LANES), BF16),
        ),
        in_specs=[pl.BlockSpec(memory_space=pltpu.HBM)] * 4,
        out_specs=(vmem, vmem),
        scratch_shapes=[
            pltpu.VMEM((dates, rows), jnp.int32),
            pltpu.VMEM((2, pair_count), jnp.int32),
            pltpu.VMEM((2, pair_count), jnp.int32),
            pltpu.VMEM(slc.shape, BF16),
            pltpu.VMEM((cols, 8 * parts), BF16),
            pltpu.SemaphoreType.DMA((6,)),
        ],
        compiler_params=pltpu.CompilerParams(vmem_limit_bytes=4 * 1024 * 1024),
        name="pack",
    )(
        *[
            pltpu.with_memory_space_constraint(x, pltpu.HBM)
            for x in (line_mask, pair_dev.T, pair_slot.T, slc)
        ]
    )
    got = lax.all_to_all(packed, "date", split_axis=0, concat_axis=0, tiled=True)
    fields = pl.pallas_call(
        functools.partial(strip_kernel, pair_count, chunk),
        out_shape=jax.ShapeDtypeStruct((parts, 32, LANES), jnp.int16),
        in_specs=[vmem] * 2,
        out_specs=vmem,
        scratch_shapes=[
            pltpu.VMEM((pairs, 16 * parts), BF16),
            pltpu.VMEM((pairs, 16 * parts), BF16),
            pltpu.VMEM((pairs, 16 * parts), BF16),
            pltpu.VMEM((8 * parts, pairs), BF16),
            pltpu.VMEM((pairs, 2 * LANES), F32),
            pltpu.VMEM((2 * pairs, 2 * LANES), BF16),
        ],
        compiler_params=pltpu.CompilerParams(vmem_limit_bytes=24 * 1024 * 1024),
        name="strip",
    )(got, table)
    back = lax.all_to_all(fields, "date", split_axis=0, concat_axis=0, tiled=True)
    out = jax.ShapeDtypeStruct((dates, rows, cols), F32)
    return pl.pallas_call(
        unpack_kernel,
        out_shape=(out, out),
        in_specs=[vmem],
        out_specs=(vmem, vmem),
        compiler_params=pltpu.CompilerParams(vmem_limit_bytes=4 * 1024 * 1024),
        name="unpack",
    )(back)


def solution(mesh):
    in_specs = (P("date", None, "grp", None), P("date", "grp"), P("date", None), P("date", None))
    out_specs = (P("date", "grp", None), P("date", "grp", None))
    return jax.shard_map(shards, mesh=mesh, in_specs=in_specs, out_specs=out_specs, check_vma=False)
```

```python
import functools

import jax
import jax.numpy as jnp
from jax import lax
from jax.experimental import pallas as pl
from jax.experimental.pallas import tpu as pltpu
from jax.sharding import PartitionSpec as P

ITERS = 2
DAMPING = 0.5
EPSILON = 1e-06
LANES = 128
HALO = 4
F32 = jnp.float32
BF16 = jnp.bfloat16


def iota(shape, dim):
    return lax.broadcasted_iota(jnp.int32, shape, dim)


def dot(a, b):
    return lax.dot_general(a, b, (((1,), (0,)), ((), ())), preferred_element_type=F32)


def split(x):
    high = x.astype(BF16)
    return high, (x - high.astype(F32)).astype(BF16)


def make_table(width, table_ref):
    blocks = LANES // width
    me = lax.axis_index("date")

    def main_place(shape, dim):
        p = iota(shape, dim)
        lane = p % LANES
        k = (lane // width - me + 64) % blocks
        line = jnp.where(k < 4, (p // LANES) * 4 + k, 1000 * (dim + 1))
        return line, lane % width

    def halo_place(shape, dim):
        p = iota(shape, dim)
        t = (p // 8 - me + 64) % 16
        j = p % 8
        return t % 8, jnp.where(j < HALO, j - HALO, width + j - HALO), t // 8

    to_line, to_col = main_place((1, 2 * LANES), 1)

    def near(line, col):
        hit = (jnp.abs(line - to_line) <= 1) & (jnp.abs(col - to_col) <= HALO)
        return hit.astype(F32)

    table_ref[0:256, :] = near(*main_place((2 * LANES, 1), 0)).astype(BF16)
    line, col, imag = halo_place((LANES, 1), 0)
    halo = near(line, col)
    table_ref[256:384, :] = halo.astype(BF16)
    table_ref[384:512, :] = (halo * (2.0 * imag.astype(F32) - 1.0)).astype(BF16)


def pack_kernel(mask_in, dev_in, slot_in, slc_in, out_ref, table_ref, mask_ref, dev_ref, slot_ref, slc_ref, side_ref, sems):
    step = slc_ref.shape[0] // 3
    copies = [
        pltpu.make_async_copy(source, target, sems.at[n])
        for n, (source, target) in enumerate(
            [(mask_in, mask_ref), (dev_in, dev_ref), (slot_in, slot_ref)]
            + [
                (slc_in.at[pl.ds(a, step)], slc_ref.at[pl.ds(a, step)])
                for a in range(0, slc_ref.shape[0], step)
            ]
        )
    ]
    for copy in copies:
        copy.start()
    parts = out_ref.shape[0]
    dates, _, rows, cols = slc_ref.shape
    width = cols // parts
    blocks = LANES // width
    make_table(width, table_ref)
    place = iota((cols, 8 * parts), 1)
    j = place % 8
    column = (place // 8) * width + jnp.where(j < HALO, j - HALO, width + j - HALO)
    side_ref[...] = (iota((cols, 8 * parts), 0) == column).astype(F32).astype(BF16)
    for copy in copies[:3]:
        copy.wait()
    mask = jnp.concatenate(
        [mask_ref[...].astype(F32), jnp.zeros((8 - dates, rows), F32)], axis=0
    )
    lane = iota((8, dates * 2 * rows), 1)
    row = iota((8, dates * 2 * rows), 0)
    picks = []
    for i in range(rows):
        for c in range(2):
            picks.append(jnp.where(lane == (row * 2 + c) * rows + i, mask[:, i : i + 1], 0.0))
    pick = jnp.concatenate(picks, axis=0).astype(BF16)
    for copy in copies[3:]:
        copy.wait()
    tiles = slc_ref[...].astype(F32).reshape(dates * 2 * rows, cols).astype(BF16)
    lines = dot(pick, tiles)
    edges = dot(lines.astype(BF16), side_ref[...])

    lane = iota((8, LANES), 1)
    row = iota((8, LANES), 0)
    block = lane // width
    block8 = lane // 8
    pair_count = dev_ref.shape[1]
    spare = jnp.zeros((2, 64 - pair_count), F32)
    index_rows = jnp.concatenate(
        [dev_ref[...].astype(F32), spare, slot_ref[...].astype(F32), spare], axis=1
    )
    index_rows = jnp.concatenate([jnp.zeros((6, LANES), F32), index_rows], axis=0)

    def rolled(array, i, c, tile, shift):
        at = (i * 2 + c) * 8
        part = array[at : at + 8, tile * LANES : (tile + 1) * LANES]
        return part if shift % LANES == 0 else pltpu.roll(part, shift % LANES, 1)

    for tile in range(cols // LANES):
        main = {
            (c, h, k): rolled(lines, 4 * h + k, c, tile, width * k)
            for c in range(2)
            for h in range(2)
            for k in range(4)
        }
        for q in range(blocks):
            e = tile * blocks + q
            groups = []
            for c in range(2):
                for h in range(2):
                    total = jnp.zeros((8, LANES), F32)
                    for k in range(4):
                        total = jnp.where(block == (q + k) % blocks, main[c, h, k], total)
                    groups.append(total)
            halo = jnp.zeros((8, LANES), F32)
            for i in range(rows):
                for c in range(2):
                    moved = rolled(edges, i, c, e // 16, 8 * (i + 8 * c))
                    halo = jnp.where(block8 == (e + i + 8 * c) % 16, moved, halo)
            for g in range(3):
                groups[g] = jnp.where(row >= 6, pltpu.roll(halo, 6 - 2 * g, 0), groups[g])
            groups[3] = jnp.where(row >= 6, index_rows, groups[3])
            out_ref[e] = jnp.concatenate(groups, axis=0).astype(BF16)


def strip_kernel(
    pair_count, chunk, got_ref, table_ref, out_ref, first_ref, second_ref, diff_ref, diff_t_ref, weight_ref, term_ref
):
    parts = got_ref.shape[0]
    slots = 8 * parts
    pairs = parts * pair_count

    got = got_ref[...].astype(F32)
    group = [got[:, 8 * g : 8 * g + 8, :] for g in range(4)]
    row = iota((parts, 8, LANES), 1)
    halo = jnp.where(
        row < 2,
        pltpu.roll(group[0], 2, 1),
        jnp.where(row < 4, pltpu.roll(group[1], 4, 1), pltpu.roll(group[2], 6, 1)),
    )
    columns = [x.reshape(slots, LANES) for x in group + [halo]]

    at = iota((2 * parts, slots), 1) - 8 * (iota((2 * parts, slots), 0) % parts)
    take = (at == 6 + iota((2 * parts, slots), 0) // parts).astype(F32).astype(BF16)
    ends = dot(take, columns[3].astype(BF16))
    ends = (8.0 * ends + pltpu.roll(ends, 64, 1)).astype(jnp.int32)
    lane = iota((parts, slots), 1)
    for k in range(pair_count):
        first = (ends[0:parts, k : k + 1] == lane).astype(F32)
        second = (ends[parts : 2 * parts, k : k + 1] == lane).astype(F32)
        at = pl.ds(k * parts, parts)
        for ref, value in ((first_ref, first), (second_ref, second), (diff_ref, second - first)):
            value = value.astype(BF16)
            ref[at, :] = jnp.concatenate([value, value], axis=1)
    diff_t_ref[...] = jnp.transpose(diff_ref[:, 0:slots].astype(F32)).astype(BF16)

    band, halo, cross = table_ref[0:256, :], table_ref[256:384, :], table_ref[384:512, :]
    band_halo = jnp.concatenate([band, band, halo, halo], axis=0)
    band_cross = jnp.concatenate([band, band, cross, cross], axis=0)

    def looks(field, edge, table):
        return dot(jnp.concatenate([*split(field), *split(edge)], axis=1), table)

    re = jnp.concatenate(columns[0:2], axis=1)
    im = jnp.concatenate(columns[2:4], axis=1)
    power_high, power_low = split(looks(re * re + im * im, columns[4] * columns[4], band_halo))
    tiles = jnp.concatenate([x.astype(BF16) for x in columns], axis=1)
    zero = jnp.zeros_like(tiles)
    both_tiles = jnp.concatenate(
        [
            jnp.concatenate([power_high, tiles[:, 0:512]], axis=1),
            jnp.concatenate([power_low, zero[:, 0:512]], axis=1),
        ],
        axis=0,
    )
    none = jnp.zeros((slots, LANES), BF16)
    halo_tiles = jnp.concatenate(
        [
            jnp.concatenate([tiles[:, 512:640], none], axis=1),
            jnp.concatenate([none, tiles[:, 512:640]], axis=1),
        ],
        axis=0,
    )

    def body(step, carry):
        at = pl.ds(pl.multiple_of(step * chunk, 16), chunk)
        u = dot(first_ref[at, :], both_tiles)
        v = dot(second_ref[at, :], both_tiles)
        u_power, u_re, u_im = u[:, 0:256], u[:, 256:512], u[:, 512:768]
        v_power, v_re, v_im = v[:, 0:256], v[:, 256:512], v[:, 512:768]
        either = jnp.concatenate([first_ref[at, 0:slots], second_ref[at, 0:slots]], axis=1)
        halos = dot(either, halo_tiles)
        u_halo, v_halo = halos[:, 0:128], halos[:, 128:256]
        real = looks(u_re * v_re + u_im * v_im, u_halo * v_halo, band_halo)
        imag = looks(u_im * v_re - u_re * v_im, u_halo * pltpu.roll(v_halo, 64, 1), band_cross)
        scale = lax.rsqrt(jnp.maximum(u_power * v_power, 1.0))
        real = real * scale
        imag = imag * scale
        weight = real * real + imag * imag
        weight_ref[at, :] = weight
        high, low = split(weight * imag)
        term_ref[at, :] = high
        term_ref[pl.ds(pl.multiple_of(pairs + step * chunk, 16), chunk), :] = low
        return carry

    if chunk == pairs:
        body(0, 0)
    else:
        lax.fori_loop(0, pairs // chunk, body, 0)

    right_side = dot(diff_t_ref[...], term_ref[0:pairs, :])
    right_side = right_side + dot(diff_t_ref[...], term_ref[pairs : 2 * pairs, :])

    def inner(a, b):
        return jnp.sum(a * b, axis=0, keepdims=True)

    half = -(-pairs // 32) * 16
    halves = (slice(0, half), slice(half, pairs))

    def operator(field):
        high, low = split(field)
        both = jnp.concatenate([high, low], axis=0)
        image = DAMPING * field
        curve = DAMPING * inner(field, field)
        for at in halves:
            spread = dot(diff_ref[at, :], both)
            term = weight_ref[at, :] * spread
            curve = curve + inner(term, spread)
            high, low = split(term)
            image = image + dot(diff_t_ref[:, at], high) + dot(diff_t_ref[:, at], low)
        return image, curve

    solution = jnp.zeros_like(right_side)
    residual = right_side
    direction = right_side
    norm_now = inner(residual, residual)
    for step in range(ITERS):
        image, curve = operator(direction)
        step_size = norm_now / (curve + EPSILON)
        solution = solution + step_size * direction
        residual = residual - step_size * image
        if step + 1 < ITERS:
            norm_next = inner(residual, residual)
            direction = residual + norm_next / (norm_now + EPSILON) * direction
            norm_now = norm_next
    pieces = []
    powers = []
    for field in (solution, residual):
        field = field.reshape(parts, 8, 2 * LANES)
        largest = jnp.max(jnp.abs(field), axis=1, keepdims=True)
        largest = jnp.maximum(largest[:, :, 0:LANES], largest[:, :, LANES : 2 * LANES])
        power = jnp.floor(jnp.log2(jnp.maximum(largest, 2.0**-126))) + 1.0
        powers.append(power)
        scale = jnp.exp2(-power)
        for h in range(2):
            part = field[:, :, h * LANES : (h + 1) * LANES]
            coded = jnp.floor(part * scale * 32768.0 + 0.5)
            coded = jnp.clip(coded, -32767.0, 32767.0).astype(jnp.int32)
            pieces += [coded[:, 2 * a : 2 * a + 2, :] for a in range(3)]
    pieces.append(jnp.concatenate(powers, axis=1).astype(jnp.int32))
    out_ref[...] = jnp.concatenate(pieces, axis=2).astype(jnp.int16)


def unpack_kernel(got_ref, *out_refs):
    parts = got_ref.shape[0]
    dates, rows, cols = out_refs[0].shape
    width = cols // parts
    blocks = LANES // width
    block = iota((8, LANES), 1) // width
    got = got_ref[...].astype(jnp.int32).astype(F32)
    none = jnp.zeros((parts, 2, LANES), F32)
    for o, out_ref in enumerate(out_refs):
        lines = [[] for _ in range(cols // LANES)]
        scale = 2.0**-15 * jnp.exp2(got[:, o : o + 1, 12 * LANES : 13 * LANES])
        for h in range(2):
            at = [(6 * o + 3 * h + a) * LANES for a in range(3)]
            part = jnp.concatenate([got[:, :, a : a + LANES] for a in at] + [none], axis=1) * scale
            for tile in range(cols // LANES):
                for k in range(4):
                    total = jnp.zeros((8, LANES), F32)
                    for q in range(blocks):
                        total = jnp.where(block == (q + k) % blocks, part[tile * blocks + q], total)
                    shift = -width * k % LANES
                    if shift:
                        total = pltpu.roll(total, shift, 1)
                    lines[tile].append(total)
        for tile in range(cols // LANES):
            whole = jnp.swapaxes(jnp.stack(lines[tile], axis=0), 0, 1)
            out_ref[:, :, tile * LANES : (tile + 1) * LANES] = whole[0:dates]


def shards(slc, line_mask, pair_dev, pair_slot):
    parts = lax.axis_size("date")
    dates, _, rows, cols = slc.shape
    pair_count = pair_dev.shape[0]
    pairs = parts * pair_count
    width = cols // parts
    chunk = max(c for c in range(16, 513, 16) if pairs % c == 0)
    vmem = pl.BlockSpec(memory_space=pltpu.VMEM)

    packed, table = pl.pallas_call(
        pack_kernel,
        out_shape=(
            jax.ShapeDtypeStruct((parts, 32, LANES), BF16),
            jax.ShapeDtypeStruct((4 * LANES, 2 * LANES), BF16),
        ),
        in_specs=[pl.BlockSpec(memory_space=pltpu.HBM)] * 4,
        out_specs=(vmem, vmem),
        scratch_shapes=[
            pltpu.VMEM((dates, rows), jnp.int32),
            pltpu.VMEM((2, pair_count), jnp.int32),
            pltpu.VMEM((2, pair_count), jnp.int32),
            pltpu.VMEM(slc.shape, BF16),
            pltpu.VMEM((cols, 8 * parts), BF16),
            pltpu.SemaphoreType.DMA((6,)),
        ],
        compiler_params=pltpu.CompilerParams(vmem_limit_bytes=4 * 1024 * 1024),
        name="pack",
    )(
        *[
            pltpu.with_memory_space_constraint(x, pltpu.HBM)
            for x in (line_mask, pair_dev.T, pair_slot.T, slc)
        ]
    )
    got = lax.all_to_all(packed, "date", split_axis=0, concat_axis=0, tiled=True)
    fields = pl.pallas_call(
        functools.partial(strip_kernel, pair_count, chunk),
        out_shape=jax.ShapeDtypeStruct((parts, 2, 13 * LANES), jnp.int16),
        in_specs=[vmem] * 2,
        out_specs=vmem,
        scratch_shapes=[
            pltpu.VMEM((pairs, 16 * parts), BF16),
            pltpu.VMEM((pairs, 16 * parts), BF16),
            pltpu.VMEM((pairs, 16 * parts), BF16),
            pltpu.VMEM((8 * parts, pairs), BF16),
            pltpu.VMEM((pairs, 2 * LANES), F32),
            pltpu.VMEM((2 * pairs, 2 * LANES), BF16),
        ],
        compiler_params=pltpu.CompilerParams(vmem_limit_bytes=24 * 1024 * 1024),
        name="strip",
    )(got, table)
    back = lax.all_to_all(fields, "date", split_axis=0, concat_axis=0, tiled=True)
    out = jax.ShapeDtypeStruct((dates, rows, cols), F32)
    return pl.pallas_call(
        unpack_kernel,
        out_shape=(out, out),
        in_specs=[vmem],
        out_specs=(vmem, vmem),
        compiler_params=pltpu.CompilerParams(vmem_limit_bytes=4 * 1024 * 1024),
        name="unpack",
    )(back)


def solution(mesh):
    in_specs = (P("date", None, "grp", None), P("date", "grp"), P("date", None), P("date", None))
    out_specs = (P("date", "grp", None), P("date", "grp", None))
    return jax.shard_map(shards, mesh=mesh, in_specs=in_specs, out_specs=out_specs, check_vma=False)
```

```python
import functools

import jax
import jax.numpy as jnp
from jax import lax
from jax.experimental import pallas as pl
from jax.experimental.pallas import tpu as pltpu
from jax.sharding import PartitionSpec as P

ITERS = 2
DAMPING = 0.5
EPSILON = 1e-06
LANES = 128
HALO = 4
F32 = jnp.float32
BF16 = jnp.bfloat16


def iota(shape, dim):
    return lax.broadcasted_iota(jnp.int32, shape, dim)


def dot(a, b):
    return lax.dot_general(a, b, (((1,), (0,)), ((), ())), preferred_element_type=F32)


def split(x):
    high = x.astype(BF16)
    return high, (x - high.astype(F32)).astype(BF16)


def make_table(width, table_ref):
    blocks = LANES // width
    me = lax.axis_index("date")

    def main_place(shape, dim):
        p = iota(shape, dim)
        lane = p % LANES
        k = (lane // width - me + 64) % blocks
        line = jnp.where(k < 4, (p // LANES) * 4 + k, 1000 * (dim + 1))
        return line, lane % width

    def halo_place(shape, dim):
        p = iota(shape, dim)
        t = (p // 8 - me + 64) % 16
        j = p % 8
        return t % 8, jnp.where(j < HALO, j - HALO, width + j - HALO), t // 8

    to_line, to_col = main_place((1, 2 * LANES), 1)

    def near(line, col):
        hit = (jnp.abs(line - to_line) <= 1) & (jnp.abs(col - to_col) <= HALO)
        return hit.astype(F32)

    table_ref[0:256, :] = near(*main_place((2 * LANES, 1), 0)).astype(BF16)
    line, col, imag = halo_place((LANES, 1), 0)
    halo = near(line, col)
    table_ref[256:384, :] = halo.astype(BF16)
    table_ref[384:512, :] = (halo * (2.0 * imag.astype(F32) - 1.0)).astype(BF16)


def pack_kernel(mask_in, dev_in, slot_in, slc_in, out_ref, table_ref, mask_ref, dev_ref, slot_ref, slc_ref, side_ref, sems):
    step = slc_ref.shape[0] // 3
    copies = [
        pltpu.make_async_copy(source, target, sems.at[n])
        for n, (source, target) in enumerate(
            [(mask_in, mask_ref), (dev_in, dev_ref), (slot_in, slot_ref)]
            + [
                (slc_in.at[pl.ds(a, step)], slc_ref.at[pl.ds(a, step)])
                for a in range(0, slc_ref.shape[0], step)
            ]
        )
    ]
    for copy in copies:
        copy.start()
    parts = out_ref.shape[0]
    dates, _, rows, cols = slc_ref.shape
    width = cols // parts
    blocks = LANES // width
    make_table(width, table_ref)
    place = iota((cols, 8 * parts), 1)
    j = place % 8
    column = (place // 8) * width + jnp.where(j < HALO, j - HALO, width + j - HALO)
    side_ref[...] = (iota((cols, 8 * parts), 0) == column).astype(F32).astype(BF16)
    for copy in copies[:3]:
        copy.wait()
    mask = mask_ref[...].astype(F32)
    diagonal = iota((rows, rows), 0) == iota((rows, rows), 1)
    valid = [
        jnp.sum(jnp.where(diagonal, mask[a : a + 1, :], 0.0), axis=1, keepdims=True)
        for a in range(dates)
    ]
    for copy in copies[3:]:
        copy.wait()
    tiles = [
        [slc_ref[a, c].astype(F32) * valid[a] for c in range(2)] for a in range(dates)
    ]
    stacked = jnp.concatenate([x for pair in tiles for x in pair], axis=0)
    edges = dot(stacked.astype(BF16), side_ref[...])
    empty = jnp.zeros((rows, LANES), F32)

    def by_line(parts_of_dates):
        whole = jnp.stack(parts_of_dates + [empty] * (8 - dates), axis=0)
        return jnp.swapaxes(whole, 0, 1)

    lines = [
        [
            by_line([tiles[a][c][:, t * LANES : (t + 1) * LANES] for a in range(dates)])
            for t in range(cols // LANES)
        ]
        for c in range(2)
    ]
    edges = [
        [
            by_line(
                [
                    edges[(2 * a + c) * rows : (2 * a + c + 1) * rows, t * LANES : (t + 1) * LANES]
                    for a in range(dates)
                ]
            )
            for t in range(8 * parts // LANES)
        ]
        for c in range(2)
    ]

    lane = iota((8, LANES), 1)
    row = iota((8, LANES), 0)
    block = lane // width
    block8 = lane // 8
    pair_count = dev_ref.shape[1]
    spare = jnp.zeros((2, 64 - pair_count), F32)
    index_rows = jnp.concatenate(
        [dev_ref[...].astype(F32), spare, slot_ref[...].astype(F32), spare], axis=1
    )
    index_rows = jnp.concatenate([jnp.zeros((6, LANES), F32), index_rows], axis=0)

    def rolled(array, i, c, tile, shift):
        part = array[c][tile][i]
        return part if shift % LANES == 0 else pltpu.roll(part, shift % LANES, 1)

    for tile in range(cols // LANES):
        main = {
            (c, h, k): rolled(lines, 4 * h + k, c, tile, width * k)
            for c in range(2)
            for h in range(2)
            for k in range(4)
        }
        for q in range(blocks):
            e = tile * blocks + q
            groups = []
            for c in range(2):
                for h in range(2):
                    total = jnp.zeros((8, LANES), F32)
                    for k in range(4):
                        total = jnp.where(block == (q + k) % blocks, main[c, h, k], total)
                    groups.append(total)
            halo = jnp.zeros((8, LANES), F32)
            for i in range(rows):
                for c in range(2):
                    moved = rolled(edges, i, c, e // 16, 8 * (i + 8 * c))
                    halo = jnp.where(block8 == (e + i + 8 * c) % 16, moved, halo)
            for g in range(3):
                groups[g] = jnp.where(row >= 6, pltpu.roll(halo, 6 - 2 * g, 0), groups[g])
            groups[3] = jnp.where(row >= 6, index_rows, groups[3])
            out_ref[e] = jnp.concatenate(groups, axis=0).astype(BF16)


def strip_kernel(
    pair_count, chunk, got_ref, table_ref, out_ref, first_ref, second_ref, diff_ref, diff_t_ref, weight_ref, term_ref
):
    parts = got_ref.shape[0]
    slots = 8 * parts
    pairs = parts * pair_count

    got = got_ref[...].astype(F32)
    group = [got[:, 8 * g : 8 * g + 8, :] for g in range(4)]
    row = iota((parts, 8, LANES), 1)
    halo = jnp.where(
        row < 2,
        pltpu.roll(group[0], 2, 1),
        jnp.where(row < 4, pltpu.roll(group[1], 4, 1), pltpu.roll(group[2], 6, 1)),
    )
    columns = [x.reshape(slots, LANES) for x in group + [halo]]

    at = iota((2 * parts, slots), 1) - 8 * (iota((2 * parts, slots), 0) % parts)
    take = (at == 6 + iota((2 * parts, slots), 0) // parts).astype(F32).astype(BF16)
    ends = dot(take, columns[3].astype(BF16))
    ends = (8.0 * ends + pltpu.roll(ends, 64, 1)).astype(jnp.int32)
    lane = iota((parts, slots), 1)
    for k in range(pair_count):
        first = (ends[0:parts, k : k + 1] == lane).astype(F32)
        second = (ends[parts : 2 * parts, k : k + 1] == lane).astype(F32)
        at = pl.ds(k * parts, parts)
        for ref, value in ((first_ref, first), (second_ref, second), (diff_ref, second - first)):
            value = value.astype(BF16)
            ref[at, :] = jnp.concatenate([value, value], axis=1)
    diff_t_ref[...] = jnp.transpose(diff_ref[:, 0:slots].astype(F32)).astype(BF16)

    band, halo, cross = table_ref[0:256, :], table_ref[256:384, :], table_ref[384:512, :]
    band_halo = jnp.concatenate([band, band, halo, halo], axis=0)
    band_cross = jnp.concatenate([band, band, cross, cross], axis=0)

    def looks(field, edge, table):
        return dot(jnp.concatenate([*split(field), *split(edge)], axis=1), table)

    re = jnp.concatenate(columns[0:2], axis=1)
    im = jnp.concatenate(columns[2:4], axis=1)
    power_high, power_low = split(looks(re * re + im * im, columns[4] * columns[4], band_halo))
    tiles = jnp.concatenate([x.astype(BF16) for x in columns], axis=1)
    zero = jnp.zeros_like(tiles)
    both_tiles = jnp.concatenate(
        [
            jnp.concatenate([power_high, tiles[:, 0:512]], axis=1),
            jnp.concatenate([power_low, zero[:, 0:512]], axis=1),
        ],
        axis=0,
    )
    none = jnp.zeros((slots, LANES), BF16)
    halo_tiles = jnp.concatenate(
        [
            jnp.concatenate([tiles[:, 512:640], none], axis=1),
            jnp.concatenate([none, tiles[:, 512:640]], axis=1),
        ],
        axis=0,
    )

    def body(step, carry):
        at = pl.ds(pl.multiple_of(step * chunk, 16), chunk)
        u = dot(first_ref[at, :], both_tiles)
        v = dot(second_ref[at, :], both_tiles)
        u_power, u_re, u_im = u[:, 0:256], u[:, 256:512], u[:, 512:768]
        v_power, v_re, v_im = v[:, 0:256], v[:, 256:512], v[:, 512:768]
        either = jnp.concatenate([first_ref[at, 0:slots], second_ref[at, 0:slots]], axis=1)
        halos = dot(either, halo_tiles)
        u_halo, v_halo = halos[:, 0:128], halos[:, 128:256]
        real = looks(u_re * v_re + u_im * v_im, u_halo * v_halo, band_halo)
        imag = looks(u_im * v_re - u_re * v_im, u_halo * pltpu.roll(v_halo, 64, 1), band_cross)
        scale = lax.rsqrt(jnp.maximum(u_power * v_power, 1.0))
        real = real * scale
        imag = imag * scale
        weight = real * real + imag * imag
        weight_ref[at, :] = weight
        high, low = split(weight * imag)
        term_ref[at, :] = high
        term_ref[pl.ds(pl.multiple_of(pairs + step * chunk, 16), chunk), :] = low
        return carry

    if chunk == pairs:
        body(0, 0)
    else:
        lax.fori_loop(0, pairs // chunk, body, 0)

    right_side = dot(diff_t_ref[...], term_ref[0:pairs, :])
    right_side = right_side + dot(diff_t_ref[...], term_ref[pairs : 2 * pairs, :])

    def inner(a, b):
        return jnp.sum(a * b, axis=0, keepdims=True)

    half = -(-pairs // 32) * 16
    halves = (slice(0, half), slice(half, pairs))

    def operator(field):
        high, low = split(field)
        both = jnp.concatenate([high, low], axis=0)
        image = DAMPING * field
        curve = DAMPING * inner(field, field)
        for at in halves:
            spread = dot(diff_ref[at, :], both)
            term = weight_ref[at, :] * spread
            curve = curve + inner(term, spread)
            high, low = split(term)
            image = image + dot(diff_t_ref[:, at], high) + dot(diff_t_ref[:, at], low)
        return image, curve

    solution = jnp.zeros_like(right_side)
    residual = right_side
    direction = right_side
    norm_now = inner(residual, residual)
    for step in range(ITERS):
        image, curve = operator(direction)
        step_size = norm_now / (curve + EPSILON)
        solution = solution + step_size * direction
        residual = residual - step_size * image
        if step + 1 < ITERS:
            norm_next = inner(residual, residual)
            direction = residual + norm_next / (norm_now + EPSILON) * direction
            norm_now = norm_next
    pieces = []
    powers = []
    for field in (solution, residual):
        field = field.reshape(parts, 8, 2 * LANES)
        largest = jnp.max(jnp.abs(field), axis=1, keepdims=True)
        largest = jnp.maximum(largest[:, :, 0:LANES], largest[:, :, LANES : 2 * LANES])
        power = jnp.floor(jnp.log2(jnp.maximum(largest, 2.0**-126))) + 1.0
        powers.append(power)
        scale = jnp.exp2(-power)
        for h in range(2):
            part = field[:, :, h * LANES : (h + 1) * LANES]
            coded = jnp.floor(part * scale * 32768.0 + 0.5)
            coded = jnp.clip(coded, -32767.0, 32767.0).astype(jnp.int32)
            pieces += [coded[:, 2 * a : 2 * a + 2, :] for a in range(3)]
    pieces.append(jnp.concatenate(powers, axis=1).astype(jnp.int32))
    out_ref[...] = jnp.concatenate(pieces, axis=2).astype(jnp.int16)


def unpack_kernel(got_ref, *out_refs):
    parts = got_ref.shape[0]
    dates, rows, cols = out_refs[0].shape
    width = cols // parts
    blocks = LANES // width
    block = iota((8, LANES), 1) // width
    got = got_ref[...].astype(jnp.int32).astype(F32)
    none = jnp.zeros((parts, 2, LANES), F32)
    for o, out_ref in enumerate(out_refs):
        lines = [[] for _ in range(cols // LANES)]
        scale = 2.0**-15 * jnp.exp2(got[:, o : o + 1, 12 * LANES : 13 * LANES])
        for h in range(2):
            at = [(6 * o + 3 * h + a) * LANES for a in range(3)]
            part = jnp.concatenate([got[:, :, a : a + LANES] for a in at] + [none], axis=1) * scale
            for tile in range(cols // LANES):
                for k in range(4):
                    total = jnp.zeros((8, LANES), F32)
                    for q in range(blocks):
                        total = jnp.where(block == (q + k) % blocks, part[tile * blocks + q], total)
                    shift = -width * k % LANES
                    if shift:
                        total = pltpu.roll(total, shift, 1)
                    lines[tile].append(total)
        for tile in range(cols // LANES):
            whole = jnp.swapaxes(jnp.stack(lines[tile], axis=0), 0, 1)
            out_ref[:, :, tile * LANES : (tile + 1) * LANES] = whole[0:dates]


def shards(slc, line_mask, pair_dev, pair_slot):
    parts = lax.axis_size("date")
    dates, _, rows, cols = slc.shape
    pair_count = pair_dev.shape[0]
    pairs = parts * pair_count
    width = cols // parts
    chunk = max(c for c in range(16, 513, 16) if pairs % c == 0)
    vmem = pl.BlockSpec(memory_space=pltpu.VMEM)

    packed, table = pl.pallas_call(
        pack_kernel,
        out_shape=(
            jax.ShapeDtypeStruct((parts, 32, LANES), BF16),
            jax.ShapeDtypeStruct((4 * LANES, 2 * LANES), BF16),
        ),
        in_specs=[pl.BlockSpec(memory_space=pltpu.HBM)] * 4,
        out_specs=(vmem, vmem),
        scratch_shapes=[
            pltpu.VMEM((dates, rows), jnp.int32),
            pltpu.VMEM((2, pair_count), jnp.int32),
            pltpu.VMEM((2, pair_count), jnp.int32),
            pltpu.VMEM(slc.shape, BF16),
            pltpu.VMEM((cols, 8 * parts), BF16),
            pltpu.SemaphoreType.DMA((6,)),
        ],
        compiler_params=pltpu.CompilerParams(vmem_limit_bytes=4 * 1024 * 1024),
        name="pack",
    )(
        *[
            pltpu.with_memory_space_constraint(x, pltpu.HBM)
            for x in (line_mask, pair_dev.T, pair_slot.T, slc)
        ]
    )
    got = lax.all_to_all(packed, "date", split_axis=0, concat_axis=0, tiled=True)
    fields = pl.pallas_call(
        functools.partial(strip_kernel, pair_count, chunk),
        out_shape=jax.ShapeDtypeStruct((parts, 2, 13 * LANES), jnp.int16),
        in_specs=[vmem] * 2,
        out_specs=vmem,
        scratch_shapes=[
            pltpu.VMEM((pairs, 16 * parts), BF16),
            pltpu.VMEM((pairs, 16 * parts), BF16),
            pltpu.VMEM((pairs, 16 * parts), BF16),
            pltpu.VMEM((8 * parts, pairs), BF16),
            pltpu.VMEM((pairs, 2 * LANES), F32),
            pltpu.VMEM((2 * pairs, 2 * LANES), BF16),
        ],
        compiler_params=pltpu.CompilerParams(vmem_limit_bytes=24 * 1024 * 1024),
        name="strip",
    )(got, table)
    back = lax.all_to_all(fields, "date", split_axis=0, concat_axis=0, tiled=True)
    out = jax.ShapeDtypeStruct((dates, rows, cols), F32)
    return pl.pallas_call(
        unpack_kernel,
        out_shape=(out, out),
        in_specs=[vmem],
        out_specs=(vmem, vmem),
        compiler_params=pltpu.CompilerParams(vmem_limit_bytes=4 * 1024 * 1024),
        name="unpack",
    )(back)


def solution(mesh):
    in_specs = (P("date", None, "grp", None), P("date", "grp"), P("date", None), P("date", None))
    out_specs = (P("date", "grp", None), P("date", "grp", None))
    return jax.shard_map(shards, mesh=mesh, in_specs=in_specs, out_specs=out_specs, check_vma=False)
```

```python
import functools

import jax
import jax.numpy as jnp
from jax import lax
from jax.experimental import pallas as pl
from jax.experimental.pallas import tpu as pltpu
from jax.sharding import PartitionSpec as P

ITERS = 2
DAMPING = 0.5
EPSILON = 1e-06
LANES = 128
HALO = 4
F32 = jnp.float32
BF16 = jnp.bfloat16


def iota(shape, dim):
    return lax.broadcasted_iota(jnp.int32, shape, dim)


def dot(a, b):
    return lax.dot_general(a, b, (((1,), (0,)), ((), ())), preferred_element_type=F32)


def split(x):
    high = x.astype(BF16)
    return high, (x - high.astype(F32)).astype(BF16)


def make_table(width, table_ref):
    blocks = LANES // width
    me = lax.axis_index("date")

    def main_place(shape, dim):
        p = iota(shape, dim)
        lane = p % LANES
        k = (lane // width - me + 64) % blocks
        line = jnp.where(k < 4, (p // LANES) * 4 + k, 1000 * (dim + 1))
        return line, lane % width

    def halo_place(shape, dim):
        p = iota(shape, dim)
        t = (p // 8 - me + 64) % 16
        j = p % 8
        return t % 8, jnp.where(j < HALO, j - HALO, width + j - HALO), t // 8

    to_line, to_col = main_place((1, 2 * LANES), 1)

    def near(line, col):
        hit = (jnp.abs(line - to_line) <= 1) & (jnp.abs(col - to_col) <= HALO)
        return hit.astype(F32)

    table_ref[0:256, :] = near(*main_place((2 * LANES, 1), 0)).astype(BF16)
    line, col, imag = halo_place((LANES, 1), 0)
    halo = near(line, col)
    table_ref[256:384, :] = halo.astype(BF16)
    table_ref[384:512, :] = (halo * (2.0 * imag.astype(F32) - 1.0)).astype(BF16)


def pack_kernel(mask_in, dev_in, slot_in, slc_in, out_ref, table_ref, mask_ref, dev_ref, slot_ref, slc_ref, side_ref, sems):
    step = slc_ref.shape[0] // 3
    copies = [
        pltpu.make_async_copy(source, target, sems.at[n])
        for n, (source, target) in enumerate(
            [(mask_in, mask_ref), (dev_in, dev_ref), (slot_in, slot_ref)]
            + [
                (slc_in.at[pl.ds(a, step)], slc_ref.at[pl.ds(a, step)])
                for a in range(0, slc_ref.shape[0], step)
            ]
        )
    ]
    for copy in copies:
        copy.start()
    parts = out_ref.shape[0]
    dates, _, rows, cols = slc_ref.shape
    width = cols // parts
    blocks = LANES // width
    make_table(width, table_ref)
    place = iota((cols, 8 * parts), 1)
    j = place % 8
    column = (place // 8) * width + jnp.where(j < HALO, j - HALO, width + j - HALO)
    side_ref[...] = (iota((cols, 8 * parts), 0) == column).astype(F32).astype(BF16)
    for copy in copies[:3]:
        copy.wait()
    mask = mask_ref[...].astype(F32)
    diagonal = iota((rows, rows), 0) == iota((rows, rows), 1)
    valid = [
        jnp.sum(jnp.where(diagonal, mask[a : a + 1, :], 0.0), axis=1, keepdims=True)
        for a in range(dates)
    ]
    for copy in copies[3:]:
        copy.wait()
    tiles = [
        [slc_ref[a, c].astype(F32) * valid[a] for c in range(2)] for a in range(dates)
    ]
    stacked = jnp.concatenate([x for pair in tiles for x in pair], axis=0)
    edges = dot(stacked.astype(BF16), side_ref[...])
    empty = jnp.zeros((rows, LANES), F32)

    def by_line(parts_of_dates):
        whole = jnp.stack(parts_of_dates + [empty] * (8 - dates), axis=0)
        return jnp.swapaxes(whole, 0, 1)

    lines = [
        [
            by_line([tiles[a][c][:, t * LANES : (t + 1) * LANES] for a in range(dates)])
            for t in range(cols // LANES)
        ]
        for c in range(2)
    ]
    edges = [
        [
            by_line(
                [
                    edges[(2 * a + c) * rows : (2 * a + c + 1) * rows, t * LANES : (t + 1) * LANES]
                    for a in range(dates)
                ]
            )
            for t in range(8 * parts // LANES)
        ]
        for c in range(2)
    ]

    lane = iota((8, LANES), 1)
    row = iota((8, LANES), 0)
    block = lane // width
    block8 = lane // 8
    pair_count = dev_ref.shape[1]
    spare = jnp.zeros((2, 64 - pair_count), F32)
    index_rows = jnp.concatenate(
        [dev_ref[...].astype(F32), spare, slot_ref[...].astype(F32), spare], axis=1
    )
    index_rows = jnp.concatenate([jnp.zeros((6, LANES), F32), index_rows], axis=0)

    def rolled(array, i, c, tile, shift):
        part = array[c][tile][i]
        return part if shift % LANES == 0 else pltpu.roll(part, shift % LANES, 1)

    for tile in range(cols // LANES):
        main = {
            (c, h, k): rolled(lines, 4 * h + k, c, tile, width * k)
            for c in range(2)
            for h in range(2)
            for k in range(4)
        }
        for q in range(blocks):
            e = tile * blocks + q
            groups = []
            for c in range(2):
                for h in range(2):
                    total = jnp.zeros((8, LANES), F32)
                    for k in range(4):
                        total = jnp.where(block == (q + k) % blocks, main[c, h, k], total)
                    groups.append(total)
            halo = jnp.zeros((8, LANES), F32)
            for i in range(rows):
                for c in range(2):
                    moved = rolled(edges, i, c, e // 16, 8 * (i + 8 * c))
                    halo = jnp.where(block8 == (e + i + 8 * c) % 16, moved, halo)
            for g in range(3):
                groups[g] = jnp.where(row >= 6, pltpu.roll(halo, 6 - 2 * g, 0), groups[g])
            groups[3] = jnp.where(row >= 6, index_rows, groups[3])
            out_ref[e] = jnp.concatenate(groups, axis=0).astype(BF16)


def strip_kernel(
    pair_count, chunk, got_ref, table_ref, out_ref, first_ref, second_ref, diff_ref, diff_t_ref, weight_ref, term_ref
):
    parts = got_ref.shape[0]
    slots = 8 * parts
    pairs = parts * pair_count

    got = got_ref[...].astype(F32)
    group = [got[:, 8 * g : 8 * g + 8, :] for g in range(4)]
    row = iota((parts, 8, LANES), 1)
    halo = jnp.where(
        row < 2,
        pltpu.roll(group[0], 2, 1),
        jnp.where(row < 4, pltpu.roll(group[1], 4, 1), pltpu.roll(group[2], 6, 1)),
    )
    columns = [x.reshape(slots, LANES) for x in group + [halo]]

    at = iota((2 * parts, slots), 1) - 8 * (iota((2 * parts, slots), 0) % parts)
    take = (at == 6 + iota((2 * parts, slots), 0) // parts).astype(F32).astype(BF16)
    ends = dot(take, columns[3].astype(BF16))
    ends = (8.0 * ends + pltpu.roll(ends, 64, 1)).astype(jnp.int32)
    lane = iota((parts, slots), 1)
    for k in range(pair_count):
        first = (ends[0:parts, k : k + 1] == lane).astype(F32)
        second = (ends[parts : 2 * parts, k : k + 1] == lane).astype(F32)
        at = pl.ds(k * parts, parts)
        for ref, value in ((first_ref, first), (second_ref, second), (diff_ref, second - first)):
            value = value.astype(BF16)
            ref[at, :] = jnp.concatenate([value, value], axis=1)
    diff_t_ref[...] = jnp.transpose(diff_ref[:, 0:slots].astype(F32)).astype(BF16)

    band, halo, cross = table_ref[0:256, :], table_ref[256:384, :], table_ref[384:512, :]
    band_halo = jnp.concatenate([band, band, halo, halo], axis=0)
    band_cross = jnp.concatenate([band, band, cross, cross], axis=0)

    def looks(field, edge, table):
        return dot(jnp.concatenate([*split(field), *split(edge)], axis=1), table)

    re = jnp.concatenate(columns[0:2], axis=1)
    im = jnp.concatenate(columns[2:4], axis=1)
    power_high, power_low = split(looks(re * re + im * im, columns[4] * columns[4], band_halo))
    tiles = jnp.concatenate([x.astype(BF16) for x in columns], axis=1)
    zero = jnp.zeros_like(tiles)
    both_tiles = jnp.concatenate(
        [
            jnp.concatenate([power_high, tiles[:, 0:512]], axis=1),
            jnp.concatenate([power_low, zero[:, 0:512]], axis=1),
        ],
        axis=0,
    )
    none = jnp.zeros((slots, LANES), BF16)
    halo_tiles = jnp.concatenate(
        [
            jnp.concatenate([tiles[:, 512:640], none], axis=1),
            jnp.concatenate([none, tiles[:, 512:640]], axis=1),
        ],
        axis=0,
    )

    def body(step, carry):
        at = pl.ds(pl.multiple_of(step * chunk, 16), chunk)
        u = dot(first_ref[at, :], both_tiles)
        v = dot(second_ref[at, :], both_tiles)
        u_power, u_re, u_im = u[:, 0:256], u[:, 256:512], u[:, 512:768]
        v_power, v_re, v_im = v[:, 0:256], v[:, 256:512], v[:, 512:768]
        either = jnp.concatenate([first_ref[at, 0:slots], second_ref[at, 0:slots]], axis=1)
        halos = dot(either, halo_tiles)
        u_halo, v_halo = halos[:, 0:128], halos[:, 128:256]
        real = looks(u_re * v_re + u_im * v_im, u_halo * v_halo, band_halo)
        imag = looks(u_im * v_re - u_re * v_im, u_halo * pltpu.roll(v_halo, 64, 1), band_cross)
        scale = lax.rsqrt(jnp.maximum(u_power * v_power, 1.0))
        real = real * scale
        imag = imag * scale
        weight = real * real + imag * imag
        weight_ref[at, :] = weight
        high, low = split(weight * imag)
        term_ref[at, :] = high
        term_ref[pl.ds(pl.multiple_of(pairs + step * chunk, 16), chunk), :] = low
        return carry

    if chunk == pairs:
        body(0, 0)
    else:
        lax.fori_loop(0, pairs // chunk, body, 0)

    right_side = dot(diff_t_ref[...], term_ref[0:pairs, :])
    right_side = right_side + dot(diff_t_ref[...], term_ref[pairs : 2 * pairs, :])

    def inner(a, b):
        return jnp.sum(a * b, axis=0, keepdims=True)

    half = -(-pairs // 32) * 16
    halves = (slice(0, half), slice(half, pairs))

    def operator(field, square):
        high, low = split(field)
        both = jnp.concatenate([high, low], axis=0)
        image = DAMPING * field
        curve = DAMPING * square
        for at in halves:
            spread = dot(diff_ref[at, :], both)
            term = weight_ref[at, :] * spread
            curve = curve + inner(term, spread)
            high, low = split(term)
            image = image + dot(diff_t_ref[:, at], high) + dot(diff_t_ref[:, at], low)
        return image, curve

    solution = jnp.zeros_like(right_side)
    residual = right_side
    direction = right_side
    norm_now = inner(residual, residual)
    square = norm_now
    for step in range(ITERS):
        image, curve = operator(direction, square)
        step_size = norm_now / (curve + EPSILON)
        solution = solution + step_size * direction
        residual = residual - step_size * image
        if step + 1 < ITERS:
            norm_next = inner(residual, residual)
            direction = residual + norm_next / (norm_now + EPSILON) * direction
            square = inner(direction, direction)
            norm_now = norm_next
    pieces = []
    powers = []
    for field in (solution, residual):
        field = field.reshape(parts, 8, 2 * LANES)
        largest = jnp.max(jnp.abs(field), axis=1, keepdims=True)
        largest = jnp.maximum(largest[:, :, 0:LANES], largest[:, :, LANES : 2 * LANES])
        power = jnp.floor(jnp.log2(jnp.maximum(largest, 2.0**-126))) + 1.0
        powers.append(power)
        scale = jnp.exp2(-power)
        for h in range(2):
            part = field[:, :, h * LANES : (h + 1) * LANES]
            coded = jnp.floor(part * scale * 32768.0 + 0.5)
            coded = jnp.clip(coded, -32767.0, 32767.0).astype(jnp.int32)
            pieces += [coded[:, 2 * a : 2 * a + 2, :] for a in range(3)]
    pieces.append(jnp.concatenate(powers, axis=1).astype(jnp.int32))
    out_ref[...] = jnp.concatenate(pieces, axis=2).astype(jnp.int16)


def unpack_kernel(got_ref, *out_refs):
    parts = got_ref.shape[0]
    dates, rows, cols = out_refs[0].shape
    width = cols // parts
    blocks = LANES // width
    block = iota((8, LANES), 1) // width
    got = got_ref[...].astype(jnp.int32).astype(F32)
    none = jnp.zeros((parts, 2, LANES), F32)
    for o, out_ref in enumerate(out_refs):
        lines = [[] for _ in range(cols // LANES)]
        scale = jnp.exp2(got[:, o : o + 1, 12 * LANES : 13 * LANES])
        for h in range(2):
            at = [(6 * o + 3 * h + a) * LANES for a in range(3)]
            part = jnp.concatenate([got[:, :, a : a + LANES] for a in at] + [none], axis=1)
            part = part * 2.0**-15 * scale
            for tile in range(cols // LANES):
                for k in range(4):
                    total = jnp.zeros((8, LANES), F32)
                    for q in range(blocks):
                        total = jnp.where(block == (q + k) % blocks, part[tile * blocks + q], total)
                    shift = -width * k % LANES
                    if shift:
                        total = pltpu.roll(total, shift, 1)
                    lines[tile].append(total)
        for tile in range(cols // LANES):
            whole = jnp.swapaxes(jnp.stack(lines[tile], axis=0), 0, 1)
            out_ref[:, :, tile * LANES : (tile + 1) * LANES] = whole[0:dates]


def shards(slc, line_mask, pair_dev, pair_slot):
    parts = lax.axis_size("date")
    dates, _, rows, cols = slc.shape
    pair_count = pair_dev.shape[0]
    pairs = parts * pair_count
    width = cols // parts
    chunk = max(c for c in range(16, 513, 16) if pairs % c == 0)
    vmem = pl.BlockSpec(memory_space=pltpu.VMEM)

    packed, table = pl.pallas_call(
        pack_kernel,
        out_shape=(
            jax.ShapeDtypeStruct((parts, 32, LANES), BF16),
            jax.ShapeDtypeStruct((4 * LANES, 2 * LANES), BF16),
        ),
        in_specs=[pl.BlockSpec(memory_space=pltpu.HBM)] * 4,
        out_specs=(vmem, vmem),
        scratch_shapes=[
            pltpu.VMEM((dates, rows), jnp.int32),
            pltpu.VMEM((2, pair_count), jnp.int32),
            pltpu.VMEM((2, pair_count), jnp.int32),
            pltpu.VMEM(slc.shape, BF16),
            pltpu.VMEM((cols, 8 * parts), BF16),
            pltpu.SemaphoreType.DMA((6,)),
        ],
        compiler_params=pltpu.CompilerParams(vmem_limit_bytes=4 * 1024 * 1024),
        name="pack",
    )(
        *[
            pltpu.with_memory_space_constraint(x, pltpu.HBM)
            for x in (line_mask, pair_dev.T, pair_slot.T, slc)
        ]
    )
    got = lax.all_to_all(packed, "date", split_axis=0, concat_axis=0, tiled=True)
    fields = pl.pallas_call(
        functools.partial(strip_kernel, pair_count, chunk),
        out_shape=jax.ShapeDtypeStruct((parts, 2, 13 * LANES), jnp.int16),
        in_specs=[vmem] * 2,
        out_specs=vmem,
        scratch_shapes=[
            pltpu.VMEM((pairs, 16 * parts), BF16),
            pltpu.VMEM((pairs, 16 * parts), BF16),
            pltpu.VMEM((pairs, 16 * parts), BF16),
            pltpu.VMEM((8 * parts, pairs), BF16),
            pltpu.VMEM((pairs, 2 * LANES), F32),
            pltpu.VMEM((2 * pairs, 2 * LANES), BF16),
        ],
        compiler_params=pltpu.CompilerParams(vmem_limit_bytes=24 * 1024 * 1024),
        name="strip",
    )(got, table)
    back = lax.all_to_all(fields, "date", split_axis=0, concat_axis=0, tiled=True)
    out = jax.ShapeDtypeStruct((dates, rows, cols), F32)
    return pl.pallas_call(
        unpack_kernel,
        out_shape=(out, out),
        in_specs=[vmem],
        out_specs=(vmem, vmem),
        compiler_params=pltpu.CompilerParams(vmem_limit_bytes=4 * 1024 * 1024),
        name="unpack",
    )(back)


def solution(mesh):
    in_specs = (P("date", None, "grp", None), P("date", "grp"), P("date", None), P("date", None))
    out_specs = (P("date", "grp", None), P("date", "grp", None))
    return jax.shard_map(shards, mesh=mesh, in_specs=in_specs, out_specs=out_specs, check_vma=False)
```

```python
import functools

import jax
import jax.numpy as jnp
from jax import lax
from jax.experimental import pallas as pl
from jax.experimental.pallas import tpu as pltpu
from jax.sharding import PartitionSpec as P

ITERS = 2
DAMPING = 0.5
EPSILON = 1e-06
LANES = 128
HALO = 4
F32 = jnp.float32
BF16 = jnp.bfloat16


def iota(shape, dim):
    return lax.broadcasted_iota(jnp.int32, shape, dim)


def dot(a, b):
    return lax.dot_general(a, b, (((1,), (0,)), ((), ())), preferred_element_type=F32)


def split(x):
    high = x.astype(BF16)
    return high, (x - high.astype(F32)).astype(BF16)


def make_table(width, table_ref):
    blocks = LANES // width
    me = lax.axis_index("date")

    def main_place(shape, dim):
        p = iota(shape, dim)
        lane = p % LANES
        k = (lane // width - me + 64) % blocks
        line = jnp.where(k < 4, (p // LANES) * 4 + k, 1000 * (dim + 1))
        return line, lane % width

    def halo_place(shape, dim):
        p = iota(shape, dim)
        t = (p // 8 - me + 64) % 16
        j = p % 8
        return t % 8, jnp.where(j < HALO, j - HALO, width + j - HALO), t // 8

    to_line, to_col = main_place((1, 2 * LANES), 1)

    def near(line, col):
        hit = (jnp.abs(line - to_line) <= 1) & (jnp.abs(col - to_col) <= HALO)
        return hit.astype(F32)

    table_ref[0:256, :] = near(*main_place((2 * LANES, 1), 0)).astype(BF16)
    line, col, imag = halo_place((LANES, 1), 0)
    halo = near(line, col)
    table_ref[256:384, :] = halo.astype(BF16)
    table_ref[384:512, :] = (halo * (2.0 * imag.astype(F32) - 1.0)).astype(BF16)


def pack_kernel(mask_in, dev_in, slot_in, slc_in, out_ref, table_ref, mask_ref, dev_ref, slot_ref, slc_ref, side_ref, sems):
    step = slc_ref.shape[0] // 3
    copies = [
        pltpu.make_async_copy(source, target, sems.at[n])
        for n, (source, target) in enumerate(
            [(mask_in, mask_ref), (dev_in, dev_ref), (slot_in, slot_ref)]
            + [
                (slc_in.at[pl.ds(a, step)], slc_ref.at[pl.ds(a, step)])
                for a in range(0, slc_ref.shape[0], step)
            ]
        )
    ]
    for n, copy in enumerate(copies):
        copy.start(priority=n % 2)
    parts = out_ref.shape[0]
    dates, _, rows, cols = slc_ref.shape
    width = cols // parts
    blocks = LANES // width
    make_table(width, table_ref)
    place = iota((cols, 8 * parts), 1)
    j = place % 8
    column = (place // 8) * width + jnp.where(j < HALO, j - HALO, width + j - HALO)
    side_ref[...] = (iota((cols, 8 * parts), 0) == column).astype(F32).astype(BF16)
    for copy in copies[:3]:
        copy.wait()
    mask = mask_ref[...].astype(F32)
    diagonal = iota((rows, rows), 0) == iota((rows, rows), 1)
    valid = [
        jnp.sum(jnp.where(diagonal, mask[a : a + 1, :], 0.0), axis=1, keepdims=True)
        for a in range(dates)
    ]
    for copy in copies[3:]:
        copy.wait()
    tiles = [
        [slc_ref[a, c].astype(F32) * valid[a] for c in range(2)] for a in range(dates)
    ]
    raw = slc_ref[...].astype(F32).reshape(dates * 2 * rows, cols).astype(BF16)
    edges = dot(raw, side_ref[...])
    empty = jnp.zeros((rows, LANES), F32)

    def by_line(parts_of_dates):
        whole = jnp.stack(parts_of_dates + [empty] * (8 - dates), axis=0)
        return jnp.swapaxes(whole, 0, 1)

    lines = [
        [
            by_line([tiles[a][c][:, t * LANES : (t + 1) * LANES] for a in range(dates)])
            for t in range(cols // LANES)
        ]
        for c in range(2)
    ]
    edges = [
        [
            by_line(
                [
                    edges[(2 * a + c) * rows : (2 * a + c + 1) * rows, t * LANES : (t + 1) * LANES]
                    * valid[a]
                    for a in range(dates)
                ]
            )
            for t in range(8 * parts // LANES)
        ]
        for c in range(2)
    ]

    lane = iota((8, LANES), 1)
    row = iota((8, LANES), 0)
    block = lane // width
    block8 = lane // 8
    pair_count = dev_ref.shape[1]
    spare = jnp.zeros((2, 64 - pair_count), F32)
    index_rows = jnp.concatenate(
        [dev_ref[...].astype(F32), spare, slot_ref[...].astype(F32), spare], axis=1
    )
    index_rows = jnp.concatenate([jnp.zeros((6, LANES), F32), index_rows], axis=0)

    def rolled(array, i, c, tile, shift):
        part = array[c][tile][i]
        return part if shift % LANES == 0 else pltpu.roll(part, shift % LANES, 1)

    for tile in range(cols // LANES):
        main = {
            (c, h, k): rolled(lines, 4 * h + k, c, tile, width * k)
            for c in range(2)
            for h in range(2)
            for k in range(4)
        }
        for q in range(blocks):
            e = tile * blocks + q
            groups = []
            for c in range(2):
                for h in range(2):
                    total = jnp.zeros((8, LANES), F32)
                    for k in range(4):
                        total = jnp.where(block == (q + k) % blocks, main[c, h, k], total)
                    groups.append(total)
            halo = jnp.zeros((8, LANES), F32)
            for i in range(rows):
                for c in range(2):
                    moved = rolled(edges, i, c, e // 16, 8 * (i + 8 * c))
                    halo = jnp.where(block8 == (e + i + 8 * c) % 16, moved, halo)
            for g in range(3):
                groups[g] = jnp.where(row >= 6, pltpu.roll(halo, 6 - 2 * g, 0), groups[g])
            groups[3] = jnp.where(row >= 6, index_rows, groups[3])
            out_ref[e] = jnp.concatenate(groups, axis=0).astype(BF16)


def strip_kernel(
    pair_count, chunk, got_ref, table_ref, out_ref, first_ref, second_ref, diff_ref, diff_t_ref, weight_ref, term_ref
):
    parts = got_ref.shape[0]
    slots = 8 * parts
    pairs = parts * pair_count

    got = got_ref[...].astype(F32)
    group = [got[:, 8 * g : 8 * g + 8, :] for g in range(4)]
    row = iota((parts, 8, LANES), 1)
    halo = jnp.where(
        row < 2,
        pltpu.roll(group[0], 2, 1),
        jnp.where(row < 4, pltpu.roll(group[1], 4, 1), pltpu.roll(group[2], 6, 1)),
    )
    columns = [x.reshape(slots, LANES) for x in group + [halo]]

    at = iota((2 * parts, slots), 1) - 8 * (iota((2 * parts, slots), 0) % parts)
    take = (at == 6 + iota((2 * parts, slots), 0) // parts).astype(F32).astype(BF16)
    ends = dot(take, columns[3].astype(BF16))
    ends = (8.0 * ends + pltpu.roll(ends, 64, 1)).astype(jnp.int32)
    lane = iota((parts, slots), 1)
    for k in range(pair_count):
        first = (ends[0:parts, k : k + 1] == lane).astype(F32)
        second = (ends[parts : 2 * parts, k : k + 1] == lane).astype(F32)
        at = pl.ds(k * parts, parts)
        for ref, value in ((first_ref, first), (second_ref, second), (diff_ref, second - first)):
            value = value.astype(BF16)
            ref[at, :] = jnp.concatenate([value, value], axis=1)
    diff_t_ref[...] = jnp.transpose(diff_ref[:, 0:slots].astype(F32)).astype(BF16)

    band, halo, cross = table_ref[0:256, :], table_ref[256:384, :], table_ref[384:512, :]
    band_halo = jnp.concatenate([band, band, halo, halo], axis=0)
    band_cross = jnp.concatenate([band, band, cross, cross], axis=0)

    def looks(field, edge, table):
        return dot(jnp.concatenate([*split(field), *split(edge)], axis=1), table)

    re = jnp.concatenate(columns[0:2], axis=1)
    im = jnp.concatenate(columns[2:4], axis=1)
    power_high, power_low = split(looks(re * re + im * im, columns[4] * columns[4], band_halo))
    tiles = jnp.concatenate([x.astype(BF16) for x in columns], axis=1)
    zero = jnp.zeros_like(tiles)
    both_tiles = jnp.concatenate(
        [
            jnp.concatenate([power_high, tiles[:, 0:512]], axis=1),
            jnp.concatenate([power_low, zero[:, 0:512]], axis=1),
        ],
        axis=0,
    )
    none = jnp.zeros((slots, LANES), BF16)
    halo_tiles = jnp.concatenate(
        [
            jnp.concatenate([tiles[:, 512:640], none], axis=1),
            jnp.concatenate([none, tiles[:, 512:640]], axis=1),
        ],
        axis=0,
    )

    half = -(-pairs // 32) * 16
    halves = (slice(0, half), slice(half, pairs))

    def scatter(high, low):
        return sum(dot(diff_t_ref[:, at], x[at]) for at in halves for x in (high, low))

    def body(step, carry):
        at = pl.ds(pl.multiple_of(step * chunk, 16), chunk)
        u = dot(first_ref[at, :], both_tiles)
        v = dot(second_ref[at, :], both_tiles)
        u_power, u_re, u_im = u[:, 0:256], u[:, 256:512], u[:, 512:768]
        v_power, v_re, v_im = v[:, 0:256], v[:, 256:512], v[:, 512:768]
        either = jnp.concatenate([first_ref[at, 0:slots], second_ref[at, 0:slots]], axis=1)
        halos = dot(either, halo_tiles)
        u_halo, v_halo = halos[:, 0:128], halos[:, 128:256]
        real = looks(u_re * v_re + u_im * v_im, u_halo * v_halo, band_halo)
        imag = looks(u_im * v_re - u_re * v_im, u_halo * pltpu.roll(v_halo, 64, 1), band_cross)
        scale = lax.rsqrt(jnp.maximum(u_power * v_power, 1.0))
        real = real * scale
        imag = imag * scale
        weight = real * real + imag * imag
        weight_ref[at, :] = weight
        high, low = split(weight * imag)
        if chunk == pairs:
            return scatter(high, low)
        term_ref[at, :] = high
        term_ref[pl.ds(pl.multiple_of(pairs + step * chunk, 16), chunk), :] = low
        return carry

    if chunk == pairs:
        right_side = body(0, 0)
    else:
        lax.fori_loop(0, pairs // chunk, body, 0)
        right_side = scatter(term_ref[0:pairs, :], term_ref[pairs : 2 * pairs, :])


    def inner(a, b):
        return jnp.sum(a * b, axis=0, keepdims=True)

    def operator(field, square):
        high, low = split(field)
        both = jnp.concatenate([high, low], axis=0)
        image = DAMPING * field
        curve = DAMPING * square
        for at in halves:
            spread = dot(diff_ref[at, :], both)
            term = weight_ref[at, :] * spread
            curve = curve + inner(term, spread)
            high, low = split(term)
            image = image + dot(diff_t_ref[:, at], high) + dot(diff_t_ref[:, at], low)
        return image, curve

    solution = jnp.zeros_like(right_side)
    residual = right_side
    direction = right_side
    norm_now = inner(residual, residual)
    square = norm_now
    for step in range(ITERS):
        image, curve = operator(direction, square)
        step_size = norm_now / (curve + EPSILON)
        solution = solution + step_size * direction
        residual = residual - step_size * image
        if step + 1 < ITERS:
            norm_next = inner(residual, residual)
            direction = residual + norm_next / (norm_now + EPSILON) * direction
            square = inner(direction, direction)
            norm_now = norm_next
    pieces = []
    powers = []
    for field in (solution, residual):
        field = field.reshape(parts, 8, 2 * LANES)
        largest = jnp.max(jnp.abs(field), axis=1, keepdims=True)
        largest = jnp.maximum(largest[:, :, 0:LANES], largest[:, :, LANES : 2 * LANES])
        power = jnp.floor(jnp.log2(jnp.maximum(largest, 2.0**-126))) + 1.0
        powers.append(power)
        scale = jnp.exp2(-power)
        for h in range(2):
            part = field[:, :, h * LANES : (h + 1) * LANES]
            coded = jnp.floor(part * scale * 32768.0 + 0.5)
            coded = jnp.clip(coded, -32767.0, 32767.0).astype(jnp.int32)
            pieces += [coded[:, 2 * a : 2 * a + 2, :] for a in range(3)]
    pieces.append(jnp.concatenate(powers, axis=1).astype(jnp.int32))
    out_ref[...] = jnp.concatenate(pieces, axis=2).astype(jnp.int16)


def unpack_kernel(got_ref, *out_refs):
    parts = got_ref.shape[0]
    dates, rows, cols = out_refs[0].shape
    width = cols // parts
    blocks = LANES // width
    block = iota((8, LANES), 1) // width
    got = got_ref[...].astype(jnp.int32).astype(F32)
    none = jnp.zeros((parts, 2, LANES), F32)
    for o, out_ref in enumerate(out_refs):
        lines = [[] for _ in range(cols // LANES)]
        scale = jnp.exp2(got[:, o : o + 1, 12 * LANES : 13 * LANES])
        for h in range(2):
            at = [(6 * o + 3 * h + a) * LANES for a in range(3)]
            part = jnp.concatenate([got[:, :, a : a + LANES] for a in at] + [none], axis=1)
            part = part * 2.0**-15 * scale
            for tile in range(cols // LANES):
                for k in range(4):
                    total = jnp.zeros((8, LANES), F32)
                    for q in range(blocks):
                        total = jnp.where(block == (q + k) % blocks, part[tile * blocks + q], total)
                    shift = -width * k % LANES
                    if shift:
                        total = pltpu.roll(total, shift, 1)
                    lines[tile].append(total)
        for tile in range(cols // LANES):
            whole = jnp.swapaxes(jnp.stack(lines[tile], axis=0), 0, 1)
            out_ref[:, :, tile * LANES : (tile + 1) * LANES] = whole[0:dates]


def shards(slc, line_mask, pair_dev, pair_slot):
    parts = lax.axis_size("date")
    dates, _, rows, cols = slc.shape
    pair_count = pair_dev.shape[0]
    pairs = parts * pair_count
    width = cols // parts
    chunk = max(c for c in range(16, 513, 16) if pairs % c == 0)
    vmem = pl.BlockSpec(memory_space=pltpu.VMEM)

    packed, table = pl.pallas_call(
        pack_kernel,
        out_shape=(
            jax.ShapeDtypeStruct((parts, 32, LANES), BF16),
            jax.ShapeDtypeStruct((4 * LANES, 2 * LANES), BF16),
        ),
        in_specs=[pl.BlockSpec(memory_space=pltpu.HBM)] * 4,
        out_specs=(vmem, vmem),
        scratch_shapes=[
            pltpu.VMEM((dates, rows), jnp.int32),
            pltpu.VMEM((2, pair_count), jnp.int32),
            pltpu.VMEM((2, pair_count), jnp.int32),
            pltpu.VMEM(slc.shape, BF16),
            pltpu.VMEM((cols, 8 * parts), BF16),
            pltpu.SemaphoreType.DMA((6,)),
        ],
        compiler_params=pltpu.CompilerParams(vmem_limit_bytes=4 * 1024 * 1024),
        name="pack",
    )(
        *[
            pltpu.with_memory_space_constraint(x, pltpu.HBM)
            for x in (line_mask, pair_dev.T, pair_slot.T, slc)
        ]
    )
    got = lax.all_to_all(packed, "date", split_axis=0, concat_axis=0, tiled=True)
    fields = pl.pallas_call(
        functools.partial(strip_kernel, pair_count, chunk),
        out_shape=jax.ShapeDtypeStruct((parts, 2, 13 * LANES), jnp.int16),
        in_specs=[vmem] * 2,
        out_specs=vmem,
        scratch_shapes=[
            pltpu.VMEM((pairs, 16 * parts), BF16),
            pltpu.VMEM((pairs, 16 * parts), BF16),
            pltpu.VMEM((pairs, 16 * parts), BF16),
            pltpu.VMEM((8 * parts, pairs), BF16),
            pltpu.VMEM((pairs, 2 * LANES), F32),
            pltpu.VMEM((2 * pairs, 2 * LANES), BF16),
        ],
        compiler_params=pltpu.CompilerParams(vmem_limit_bytes=24 * 1024 * 1024),
        name="strip",
    )(got, table)
    back = lax.all_to_all(fields, "date", split_axis=0, concat_axis=0, tiled=True)
    out = jax.ShapeDtypeStruct((dates, rows, cols), F32)
    return pl.pallas_call(
        unpack_kernel,
        out_shape=(out, out),
        in_specs=[vmem],
        out_specs=(vmem, vmem),
        compiler_params=pltpu.CompilerParams(vmem_limit_bytes=4 * 1024 * 1024),
        name="unpack",
    )(back)


def solution(mesh):
    in_specs = (P("date", None, "grp", None), P("date", "grp"), P("date", None), P("date", None))
    out_specs = (P("date", "grp", None), P("date", "grp", None))
    return jax.shard_map(shards, mesh=mesh, in_specs=in_specs, out_specs=out_specs, check_vma=False)
```
